32 devices in a mesh: groups: 2 (over y), patch: 16 (over z, x, core).
Axes of the slice: x: 2, y: 2, z: 4, core: 2. Of those that a mesh axis runs over, the one named last changes fastest.
Arguments:
- queries: bfloat16 [2, 768, 4096], P(None, ('groups', 'patch')), parts along dimension 1, may hold values from -44 to 44
- current_pairs: bfloat16 [2, 2, 768, 4096], P(None, None, ('groups', 'patch')), parts along dimension 2, may hold values from -5 to 5
- earlier_pairs: bfloat16 [2, 2, 768, 4096], P(None, None, ('groups', 'patch')), parts along dimension 2, may hold values from -5 to 5
- stale_cache: bfloat16 [2, 2, 32, 16, 24, 256], P(None, None, ('groups', 'patch')), parts along dimension 2, may hold values from -4 to 4
- block_exponents: int32 [2, 2, 768, 32], P(None, None, ('groups', 'patch')), parts along dimension 2, may hold values from 0 to 8
- step_index: int32 [2], P('groups'), parts along dimension 0, may hold values from 0 to 49
Outputs:
- attended: bfloat16 [2, 768, 4096], P(None, ('groups', 'patch')), parts along dimension 1
- renewed_cache: bfloat16 [2, 2, 32, 16, 24, 256], P(None, None, ('groups', 'patch')), parts along dimension 2
The draws below stay inside these ranges and needn't reach their ends.
There are 2 independent parts, one for each index of `groups`. The reference program is written for one: setup_inputs(seed, part) draws one part's arguments, and reference() takes and returns one part's arrays. A program takes and returns all parts, laid end to end along the dimension named above; each array names one. Nothing has to cross between parts.
All inputs are finite; a program needn't handle non-finite values.
Results may differ from the reference program's by a relative error of at most 0.0086.
Values may be sent and summed in bfloat16 or wider, within the bound.
No kernel may reach another device: no remote copies, remote signals or barrier semaphores. Data moves between devices by JAX's collectives and lax.ppermute only.
A program may use at most 64 MiB of HBM per device.

```python
import math
import jax
import jax.numpy as jnp
import numpy as np
from jax import lax

LAYERS = 2
HEADS = 32
HEAD_DIM = 128
STEPS = 50
HEAD_GROUPS = 16
KEY_PARTS = 1
GROUP_HEADS = 2
PART_ROWS = 24
TOKENS = 384
N_PATCH = 16


def unit_draw(key, salt, shape):
    return jax.random.uniform(jax.random.fold_in(key, salt), shape, jnp.float32, 1e-06, 1.0 - 1e-06)


def gauss_from(units, partner, bound):
    radius = jnp.sqrt(-2.0 * jnp.log(units))
    return jnp.clip(radius * jnp.cos(2.0 * math.pi * partner), -bound, bound)


def pair_shape():
    return (LAYERS, 2, TOKENS, HEADS * HEAD_DIM)


def key_units(key):
    return unit_draw(key, 11, pair_shape())


def fresh_units(key):
    return unit_draw(key, 23, pair_shape())


def owner_layout(values):
    shaped = values.reshape(LAYERS, 2, N_PATCH, KEY_PARTS, PART_ROWS, HEAD_GROUPS, GROUP_HEADS * HEAD_DIM)
    return shaped.transpose(0, 1, 5, 3, 2, 4, 6).reshape(LAYERS, 2, N_PATCH, N_PATCH, PART_ROWS, GROUP_HEADS * HEAD_DIM)


def draw_stale_cache(key, part):
    units = key_units(key)
    key = jax.random.fold_in(key, 3)
    values = gauss_from(units, unit_draw(key, 31, pair_shape()), 4.0)
    return owner_layout(values).astype(jnp.bfloat16)


def draw_queries(key, part):
    key = jax.random.fold_in(key, 5)
    own_units = unit_draw(key, 1, (LAYERS, TOKENS, HEADS * HEAD_DIM))
    partner = unit_draw(key, 33, (LAYERS, TOKENS, HEADS * HEAD_DIM))
    values = 1.5 * gauss_from(own_units, partner, 4.0)
    return values.astype(jnp.bfloat16)


def draw_current_pairs(key, part):
    units = fresh_units(key)
    key = jax.random.fold_in(key, 7)
    values = gauss_from(units, unit_draw(key, 35, pair_shape()), 5.0)
    return values.astype(jnp.bfloat16)


def draw_earlier_pairs(key, part):
    key = jax.random.fold_in(key, 9)
    own_units = unit_draw(key, 2, pair_shape())
    values = gauss_from(own_units, unit_draw(key, 37, pair_shape()), 5.0)
    return values.astype(jnp.bfloat16)


def plant(entries, key, least, top_value):
    spot = [jax.random.randint(jax.random.fold_in(key, axis), (), 0, length) for axis, length in enumerate(entries.shape)]
    longest = entries.shape.index(max(entries.shape))
    next_to = spot[:longest] + [(spot[longest] + 1) % entries.shape[longest]] + spot[longest + 1:]
    return entries.at[tuple(spot)].set(least).at[tuple(next_to)].set(top_value)


def setup_inputs(seed: int = 0, part: int = 0) -> dict:
    splits = jax.random.split(jax.random.key(seed), 7)
    part_splits = jax.random.split(jax.random.fold_in(splits[6], part), 7)
    queries = draw_queries(jax.random.fold_in(jax.random.fold_in(splits[6], part), 71), part)
    current_pairs = draw_current_pairs(jax.random.fold_in(jax.random.fold_in(splits[6], part), 71), part)
    earlier_pairs = draw_earlier_pairs(jax.random.fold_in(jax.random.fold_in(splits[6], part), 71), part)
    stale_cache = draw_stale_cache(jax.random.fold_in(jax.random.fold_in(splits[6], part), 71), part)
    block_exponents = plant(jax.random.randint(part_splits[4], (LAYERS, 2, TOKENS, HEADS), 0, 9), jax.random.fold_in(part_splits[4], 1), 0, 8).astype(jnp.int32)
    step_index = jax.random.randint(part_splits[5], (1,), 0, STEPS).astype(jnp.int32)
    return dict(queries=queries, current_pairs=current_pairs, earlier_pairs=earlier_pairs, stale_cache=stale_cache, block_exponents=block_exponents, step_index=step_index)


saturation = 448.0
level_count = 9
gain_table = np.array([2.0 ** power for power in range(level_count)])
shrink_table = np.array([2.0 ** (-power) for power in range(level_count)])


def table_lookup(exponents, table):
    levels = jnp.arange(level_count, dtype=jnp.int32)
    values = jnp.asarray(table, dtype=jnp.float32)
    return jnp.sum(jnp.where(exponents[..., None] == levels, values, 0.0), -1)


def owner_to_tokens(cache):
    shaped = cache.reshape(LAYERS, 2, HEAD_GROUPS, KEY_PARTS, N_PATCH, PART_ROWS, GROUP_HEADS * HEAD_DIM)
    return shaped.transpose(0, 1, 4, 3, 5, 2, 6).reshape(LAYERS, 2, TOKENS, HEADS * HEAD_DIM)


def tokens_to_owner(pairs):
    shaped = pairs.reshape(LAYERS, 2, N_PATCH, KEY_PARTS, PART_ROWS, HEAD_GROUPS, GROUP_HEADS * HEAD_DIM)
    return shaped.transpose(0, 1, 5, 3, 2, 4, 6).reshape(LAYERS, 2, N_PATCH, N_PATCH, PART_ROWS, GROUP_HEADS * HEAD_DIM)


def one_head(operands):
    query_rows, key_rows, value_rows = operands
    score_scale = HEAD_DIM ** -0.5
    scores = jnp.einsum("qd,rkd->rqk", query_rows, key_rows) * score_scale
    row_peak = jnp.max(scores, -1, keepdims=True)
    weights = jnp.exp(scores - row_peak)
    row_total = jnp.sum(weights, -1)
    probs = lax.optimization_barrier(weights.astype(jnp.bfloat16)).astype(jnp.float32)
    partial_out = jnp.einsum("rqk,rkd->rqd", probs, value_rows) / row_total[..., None]
    log_total = row_peak[..., 0] + jnp.log(row_total)
    highest = jnp.max(log_total, 0, keepdims=True)
    factor = jnp.exp(log_total - highest)
    return jnp.sum(factor[..., None] * partial_out, 0) / jnp.sum(factor, 0)[..., None]


def split_keys(block):
    shaped = block.astype(jnp.float32).reshape(N_PATCH, KEY_PARTS, PART_ROWS, HEADS, HEAD_DIM)
    return shaped.transpose(3, 1, 0, 2, 4).reshape(HEADS, KEY_PARTS, N_PATCH * PART_ROWS, HEAD_DIM)


def attend_layer(query_block, key_block, value_block):
    query_heads = query_block.astype(jnp.float32).reshape(TOKENS, HEADS, HEAD_DIM).transpose(1, 0, 2)
    result = lax.map(one_head, (query_heads, split_keys(key_block), split_keys(value_block)))
    return result.transpose(1, 0, 2).reshape(TOKENS, HEADS * HEAD_DIM).astype(jnp.bfloat16)


def reference(queries, current_pairs, earlier_pairs, stale_cache, block_exponents, step_index):
    gains = table_lookup(block_exponents, gain_table)
    shrinks = table_lookup(block_exponents, shrink_table)
    residual = (current_pairs.astype(jnp.float32) - earlier_pairs.astype(jnp.float32)).reshape(LAYERS, 2, TOKENS, HEADS, HEAD_DIM)
    coded = lax.optimization_barrier(jnp.clip(residual * gains[..., None], -saturation, saturation).astype(jnp.bfloat16))
    update = lax.optimization_barrier((coded.astype(jnp.float32) * shrinks[..., None]).astype(jnp.bfloat16))
    update = update.reshape(LAYERS, 2, TOKENS, HEADS * HEAD_DIM)
    refresh = (step_index[0] % 2 != jnp.arange(LAYERS, dtype=jnp.int32) % 2).astype(jnp.float32)
    blend = 1.0 - step_index[0].astype(jnp.float32) / (2.0 * STEPS)
    weight = refresh * blend
    cached = owner_to_tokens(stale_cache)
    renewed = (cached.astype(jnp.float32) + weight[:, None, None, None] * update.astype(jnp.float32)).astype(jnp.bfloat16)
    attended = jnp.stack([attend_layer(queries[index], renewed[index, 0], renewed[index, 1]) for index in range(LAYERS)])
    return attended, tokens_to_owner(renewed)
```

```python
from functools import partial

import jax
import jax.numpy as jnp
from jax import lax
from jax.experimental import pallas as pl
from jax.experimental.pallas import tpu as pltpu
from jax.sharding import PartitionSpec as P

STEPS = 50
SATURATION = 448
TOP_LEVEL = 8
VMEM_BYTES = 40 * 1024 * 1024


def block_limits(exponents):
    return ((SATURATION << TOP_LEVEL) >> exponents).astype(jnp.float32) * (2.0**-TOP_LEVEL)


def blend_of(step):
    return 1.0 - step.astype(jnp.float32) / (2.0 * STEPS)


def exchange(rows):
    return lax.all_to_all(rows, "patch", split_axis=0, concat_axis=0, tiled=True)


def pack_kernel(step_ref, query_ref, current_ref, earlier_ref, exponent_ref, out_ref):
    layer_count = query_ref.shape[0]
    devices, _, _ = out_ref.shape
    head_count = exponent_ref.shape[-1]
    channel_count = query_ref.shape[-1]
    head_dim = channel_count // head_count
    width = channel_count // devices
    for layer in range(layer_count):
        for device in range(devices):
            out_ref[device, :, layer * width : (layer + 1) * width] = query_ref[
                layer, :, device * width : (device + 1) * width
            ]
    for side in range(2):
        limits = block_limits(exponent_ref[0, side])
        first = (layer_count + side) * width
        for head in range(head_count):
            span = slice(head * head_dim, (head + 1) * head_dim)
            residual = current_ref[0, side, :, span].astype(jnp.float32) - earlier_ref[
                0, side, :, span
            ].astype(jnp.float32)
            limit = limits[:, head : head + 1]
            update = jnp.minimum(jnp.maximum(residual, -limit), limit).astype(jnp.bfloat16)
            device, inner = divmod(head * head_dim, width)
            out_ref[device, :, first + inner : first + inner + head_dim] = update


def pack(step_index, queries, current_pairs, earlier_pairs, block_exponents, devices):
    layer_count, token_count, channel_count = queries.shape
    head_count = block_exponents.shape[-1]
    width = channel_count // devices

    def renewed_layer(i, step):
        return (1 - lax.rem(step[0], 2), 0, 0, 0)

    pair_spec = pl.BlockSpec((1, 2, token_count, channel_count), renewed_layer)
    return pl.pallas_call(
        pack_kernel,
        grid_spec=pltpu.PrefetchScalarGridSpec(
            num_scalar_prefetch=1,
            grid=(1,),
            in_specs=[
                pl.BlockSpec(queries.shape, lambda i, step: (0, 0, 0)),
                pair_spec,
                pair_spec,
                pl.BlockSpec((1, 2, token_count, head_count), renewed_layer),
            ],
            out_specs=pl.BlockSpec(
                (devices, token_count, (layer_count + 2) * width), lambda i, step: (0, 0, 0)
            ),
        ),
        out_shape=jax.ShapeDtypeStruct(
            (devices, token_count, (layer_count + 2) * width), jnp.bfloat16
        ),
        compiler_params=pltpu.CompilerParams(vmem_limit_bytes=VMEM_BYTES),
    )(step_index, queries, current_pairs, earlier_pairs, block_exponents)


def attend_kernel(head_dim, step_ref, arrived_ref, stale_ref, out_ref, renewed_ref):
    layer_count = stale_ref.shape[0]
    width = stale_ref.shape[-1]
    step = step_ref[0]
    blend = blend_of(step)
    score_scale = head_dim ** (-0.5)
    for layer in range(layer_count):
        weight = jnp.where(lax.rem(step, 2) != layer % 2, blend, 0.0)
        rows = []
        for side in range(2):
            first = (layer_count + side) * width
            update = arrived_ref[:, first : first + width].astype(jnp.float32)
            renewed = (stale_ref[layer, side].astype(jnp.float32) + weight * update).astype(
                jnp.bfloat16
            )
            renewed_ref[layer, side] = renewed
            rows.append(renewed)
        for head in range(width // head_dim):
            span = slice(head * head_dim, (head + 1) * head_dim)
            place = slice(layer * width + head * head_dim, layer * width + (head + 1) * head_dim)
            scores = lax.dot_general(
                arrived_ref[:, place],
                rows[0][:, span],
                (((1,), (1,)), ((), ())),
                preferred_element_type=jnp.float32,
            )
            peak = jnp.max(scores, -1, keepdims=True)
            weights = jnp.exp((scores - peak) * score_scale)
            total = jnp.sum(weights, -1, keepdims=True)
            mixed = jnp.dot(
                weights.astype(jnp.bfloat16),
                rows[1][:, span],
                preferred_element_type=jnp.float32,
            )
            out_ref[:, place] = (mixed / total).astype(jnp.bfloat16)


def attend(step_index, arrived, stale, head_dim):
    layer_count, _, row_count, width = stale.shape
    whole = pl.BlockSpec(memory_space=pltpu.VMEM)
    return pl.pallas_call(
        partial(attend_kernel, head_dim),
        in_specs=[pl.BlockSpec(memory_space=pltpu.SMEM), whole, whole],
        out_specs=[whole, whole],
        out_shape=[
            jax.ShapeDtypeStruct((row_count, layer_count * width), jnp.bfloat16),
            jax.ShapeDtypeStruct(stale.shape, jnp.bfloat16),
        ],
        compiler_params=pltpu.CompilerParams(vmem_limit_bytes=VMEM_BYTES),
    )(step_index, arrived, stale)


def whole_key_body(
    queries, current_pairs, earlier_pairs, stale_cache, block_exponents, step_index
):
    devices = lax.axis_size("patch")
    layer_count, token_count, channel_count = queries.shape
    head_dim = channel_count // block_exponents.shape[-1]
    width = channel_count // devices
    packed = pack(
        step_index, queries, current_pairs, earlier_pairs, block_exponents, devices
    )
    arrived = exchange(packed.reshape(devices * token_count, -1))
    stale = stale_cache.reshape(layer_count, 2, devices * token_count, width)
    partial_out, renewed = attend(step_index, arrived, stale, head_dim)
    back = exchange(partial_out)
    attended = (
        back.reshape(devices, token_count, layer_count, width)
        .transpose(2, 1, 0, 3)
        .reshape(layer_count, token_count, channel_count)
    )
    return attended, renewed.reshape(stale_cache.shape)


def answer_part(blocks, key_rows, value_rows):
    score_scale = key_rows.shape[-1] ** (-0.5)

    def one_block(query_block):
        scores = (
            jnp.einsum("qhd,khd->hqk", query_block, key_rows, preferred_element_type=jnp.float32)
            * score_scale
        )
        peak = jnp.max(scores, -1, keepdims=True)
        weights = jnp.exp(scores - peak)
        total = jnp.sum(weights, -1)
        mixed = jnp.einsum(
            "hqk,khd->qhd",
            weights.astype(jnp.bfloat16),
            value_rows,
            preferred_element_type=jnp.float32,
        )
        return mixed / total.T[..., None], (peak[..., 0] + jnp.log(total)).T

    return lax.map(one_block, blocks)


def split_key_body(
    queries, current_pairs, earlier_pairs, stale_cache, block_exponents, step_index
):
    devices = lax.axis_size("patch")
    layer_count, token_count, channel_count = queries.shape
    head_count = block_exponents.shape[-1]
    head_dim = channel_count // head_count
    group_count = min(head_count, devices)
    part_count = devices // group_count
    group_heads = head_count // group_count
    part_rows = token_count // part_count
    width = group_heads * head_dim
    selector = step_index[0] % 2
    blend = blend_of(step_index[0])
    limits = block_limits(block_exponents)[..., None]
    residual = (current_pairs.astype(jnp.float32) - earlier_pairs.astype(jnp.float32)).reshape(
        layer_count, 2, token_count, head_count, head_dim
    )
    update = jnp.clip(residual, -limits, limits).astype(jnp.bfloat16)
    pieces = update.reshape(layer_count, 2, part_count, part_rows, group_count, width)
    pieces = pieces.transpose(0, 4, 2, 1, 3, 5).reshape(
        layer_count, devices, 2 * part_rows, width
    )
    asked = queries.reshape(layer_count, token_count, group_count, 1, width)
    asked = jnp.broadcast_to(
        asked.transpose(0, 2, 3, 1, 4),
        (layer_count, group_count, part_count, token_count, width),
    ).reshape(layer_count, devices, token_count, width)
    attended_list = []
    renewed_list = []
    for layer in range(layer_count):
        refresh = selector != layer % 2
        outgoing = jnp.where(refresh, pieces[layer], jnp.zeros_like(pieces[layer]))
        arrived = exchange(jnp.concatenate([outgoing, asked[layer]], 1))
        arrived_update = arrived[:, : 2 * part_rows].reshape(devices, 2, part_rows, width)
        renewed = (
            stale_cache[layer, :, 0].astype(jnp.float32)
            + blend * arrived_update.transpose(1, 0, 2, 3).astype(jnp.float32)
        ).astype(jnp.bfloat16)
        key_rows = renewed[0].reshape(devices * part_rows, group_heads, head_dim)
        value_rows = renewed[1].reshape(devices * part_rows, group_heads, head_dim)
        block_span = 1
        while (
            block_span * token_count < 512 and devices % (2 * block_span) == 0
        ):
            block_span = block_span * 2
        blocks = arrived[:, 2 * part_rows :].reshape(
            devices // block_span, block_span * token_count, group_heads, head_dim
        )
        partial_out, log_total = answer_part(blocks, key_rows, value_rows)
        back_out = exchange(
            partial_out.astype(jnp.bfloat16).reshape(devices, token_count, width)
        ).astype(jnp.float32)
        back_log = exchange(
            log_total.astype(jnp.bfloat16).reshape(devices, token_count, group_heads)
        ).astype(jnp.float32)
        back_out = back_out.reshape(group_count, part_count, token_count, group_heads, head_dim)
        back_log = back_log.reshape(group_count, part_count, token_count, group_heads)
        factor = jnp.exp(back_log - jnp.max(back_log, 1, keepdims=True))
        merged = jnp.sum(factor[..., None] * back_out, 1) / jnp.sum(factor, 1)[..., None]
        attended_list.append(
            merged.transpose(1, 0, 2, 3)
            .reshape(token_count, channel_count)
            .astype(jnp.bfloat16)
        )
        renewed_list.append(renewed)
    return jnp.stack(attended_list), jnp.stack(renewed_list)[:, :, None]


def body(queries, current_pairs, earlier_pairs, stale_cache, block_exponents, step_index):
    layer_count = queries.shape[0]
    head_count = block_exponents.shape[-1]
    one_part = lax.axis_size("patch") <= head_count and layer_count == 2
    chosen = whole_key_body if one_part else split_key_body
    return chosen(
        queries, current_pairs, earlier_pairs, stale_cache, block_exponents, step_index
    )


def solution(mesh):
    in_specs = (
        P(None, ("groups", "patch"), None),
        P(None, None, ("groups", "patch"), None),
        P(None, None, ("groups", "patch"), None),
        P(None, None, ("groups", "patch"), None, None, None),
        P(None, None, ("groups", "patch"), None),
        P("groups"),
    )
    out_specs = (
        P(None, ("groups", "patch"), None),
        P(None, None, ("groups", "patch"), None, None, None),
    )
    return jax.shard_map(body, mesh=mesh, in_specs=in_specs, out_specs=out_specs, check_vma=False)
```

```python
from functools import partial

import jax
import jax.numpy as jnp
from jax import lax
from jax.experimental import pallas as pl
from jax.experimental.pallas import tpu as pltpu
from jax.sharding import PartitionSpec as P

STEPS = 50
SATURATION = 448
TOP_LEVEL = 8
VMEM_BYTES = 40 * 1024 * 1024
PACK_BYTES = 60 * 1024 * 1024


def block_limits(exponents):
    return ((SATURATION << TOP_LEVEL) >> exponents).astype(jnp.float32) * (2.0**-TOP_LEVEL)


def blend_of(step):
    return 1.0 - step.astype(jnp.float32) / (2.0 * STEPS)


def exchange(rows):
    return lax.all_to_all(rows, "patch", split_axis=0, concat_axis=0, tiled=True)


def pack_kernel(
    step_ref,
    query_ref,
    current_ref,
    earlier_ref,
    exponent_ref,
    packed_ref,
    weight_ref,
    queries,
    current,
    earlier,
    exponents,
    sems,
):
    layer_count, _, channel_count = query_ref.shape
    devices = packed_ref.shape[0]
    head_count = exponent_ref.shape[-1]
    head_dim = channel_count // head_count
    width = channel_count // devices
    step = step_ref[0]
    renewed_layer = 1 - lax.rem(step, 2)
    pairs = (
        (query_ref, queries),
        (current_ref.at[renewed_layer], current),
        (earlier_ref.at[renewed_layer], earlier),
        (exponent_ref.at[renewed_layer], exponents),
    )
    copies = [
        pltpu.make_async_copy(source, target, sems.at[index])
        for index, (source, target) in enumerate(pairs)
    ]
    for copy in copies:
        copy.start()
    for layer in range(layer_count):
        weight = jnp.where(lax.rem(step, 2) != layer % 2, blend_of(step), 0.0)
        weight_ref[layer] = jnp.zeros(weight_ref.shape[1:], jnp.float32) + weight
    copies[0].wait()
    for layer in range(layer_count):
        for device in range(devices):
            packed_ref[device, :, layer * width : (layer + 1) * width] = queries[
                layer, :, device * width : (device + 1) * width
            ]
    for copy in copies[1:]:
        copy.wait()
    for side in range(2):
        limits = block_limits(exponents[side])
        first = (layer_count + side) * width
        for head in range(head_count):
            span = slice(head * head_dim, (head + 1) * head_dim)
            residual = current[side, :, span].astype(jnp.float32) - earlier[
                side, :, span
            ].astype(jnp.float32)
            limit = limits[:, head : head + 1]
            update = jnp.minimum(jnp.maximum(residual, -limit), limit).astype(jnp.bfloat16)
            device, inner = divmod(head * head_dim, width)
            packed_ref[device, :, first + inner : first + inner + head_dim] = update


def pack(step_index, queries, current_pairs, earlier_pairs, block_exponents, devices):
    layer_count, token_count, channel_count = queries.shape
    width = channel_count // devices
    far = pl.BlockSpec(memory_space=pl.ANY)
    packed = jax.ShapeDtypeStruct(
        (devices, token_count, (layer_count + 2) * width), jnp.bfloat16
    )
    layers = [current_pairs, earlier_pairs, block_exponents]
    return pl.pallas_call(
        pack_kernel,
        in_specs=[pl.BlockSpec(memory_space=pltpu.SMEM)] + [far] * 4,
        out_specs=[pl.BlockSpec(memory_space=pltpu.VMEM)]*2,
        out_shape=[packed, jax.ShapeDtypeStruct((layer_count, 8, 128), jnp.float32)],
        scratch_shapes=[pltpu.VMEM(queries.shape, queries.dtype)]
        + [pltpu.VMEM(array.shape[1:], array.dtype) for array in layers]
        + [
            pltpu.SemaphoreType.DMA((4,)),
        ],
        compiler_params=pltpu.CompilerParams(vmem_limit_bytes=PACK_BYTES),
    )(step_index, queries, current_pairs, earlier_pairs, block_exponents)


def attend_kernel(
    head_dim, weight_ref, arrived_ref, stale_ref, out_ref, renewed_out, renewed_ref, sems
):
    layer_count = stale_ref.shape[0]
    width = stale_ref.shape[-1]
    score_scale = head_dim ** (-0.5)
    copies = []
    for layer in range(layer_count):
        weight = weight_ref[layer, 0:1, 0:1]
        rows = []
        for side in range(2):
            first = (layer_count + side) * width
            update = arrived_ref[:, first : first + width].astype(jnp.float32)
            renewed = (stale_ref[layer, side].astype(jnp.float32) + weight * update).astype(
                jnp.bfloat16
            )
            renewed_ref[layer, side] = renewed
            rows.append(renewed)
        copies.append(
            pltpu.make_async_copy(
                renewed_ref.at[layer], renewed_out.at[layer], sems.at[layer]
            )
        )
        copies[-1].start()
        for head in range(width // head_dim):
            span = slice(head * head_dim, (head + 1) * head_dim)
            place = slice(layer * width + head * head_dim, layer * width + (head + 1) * head_dim)
            scores = lax.dot_general(
                arrived_ref[:, place],
                rows[0][:, span],
                (((1,), (1,)), ((), ())),
                preferred_element_type=jnp.float32,
            )
            peak = jnp.max(scores, -1, keepdims=True)
            weights = jnp.exp((scores - peak) * score_scale)
            total = jnp.sum(weights, -1, keepdims=True)
            mixed = jnp.dot(
                weights.astype(jnp.bfloat16),
                rows[1][:, span],
                preferred_element_type=jnp.float32,
            )
            out_ref[:, layer, :, span] = (
                (mixed / total)
                .reshape(out_ref.shape[0], out_ref.shape[2], head_dim)
                .astype(jnp.bfloat16)
            )
    for copy in copies:
        copy.wait()


def attend(weights, arrived, stale, devices, head_dim):
    layer_count, _, row_count, width = stale.shape
    whole = pl.BlockSpec(memory_space=pltpu.VMEM)
    return pl.pallas_call(
        partial(attend_kernel, head_dim),
        in_specs=[whole] * 3,
        out_specs=[whole, pl.BlockSpec(memory_space=pl.ANY)],
        out_shape=[
            jax.ShapeDtypeStruct(
                (devices, layer_count, row_count // devices, width), jnp.bfloat16
            ),
            jax.ShapeDtypeStruct(stale.shape, jnp.bfloat16),
        ],
        scratch_shapes=[
            pltpu.VMEM(stale.shape, jnp.bfloat16),
            pltpu.SemaphoreType.DMA((layer_count,)),
        ],
        compiler_params=pltpu.CompilerParams(vmem_limit_bytes=VMEM_BYTES),
    )(weights, arrived, stale)


def whole_key_body(
    queries, current_pairs, earlier_pairs, stale_cache, block_exponents, step_index
):
    devices = lax.axis_size("patch")
    layer_count, token_count, channel_count = queries.shape
    head_dim = channel_count // block_exponents.shape[-1]
    width = channel_count // devices
    packed, weights = pack(
        step_index, queries, current_pairs, earlier_pairs, block_exponents, devices
    )
    arrived = exchange(packed.reshape(devices * token_count, -1))
    stale = stale_cache.reshape(layer_count, 2, devices * token_count, width)
    partial_out, renewed = attend(weights, arrived, stale, devices, head_dim)
    back = exchange(partial_out)
    attended = back.transpose(1, 2, 0, 3).reshape(layer_count, token_count, channel_count)
    return attended, renewed.reshape(stale_cache.shape)


def answer_part(blocks, key_rows, value_rows):
    score_scale = key_rows.shape[-1] ** (-0.5)

    def one_block(query_block):
        scores = (
            jnp.einsum("qhd,khd->hqk", query_block, key_rows, preferred_element_type=jnp.float32)
            * score_scale
        )
        peak = jnp.max(scores, -1, keepdims=True)
        weights = jnp.exp(scores - peak)
        total = jnp.sum(weights, -1)
        mixed = jnp.einsum(
            "hqk,khd->qhd",
            weights.astype(jnp.bfloat16),
            value_rows,
            preferred_element_type=jnp.float32,
        )
        return mixed / total.T[..., None], (peak[..., 0] + jnp.log(total)).T

    return lax.map(one_block, blocks)


def split_key_body(
    queries, current_pairs, earlier_pairs, stale_cache, block_exponents, step_index
):
    devices = lax.axis_size("patch")
    layer_count, token_count, channel_count = queries.shape
    head_count = block_exponents.shape[-1]
    head_dim = channel_count // head_count
    group_count = min(head_count, devices)
    part_count = devices // group_count
    group_heads = head_count // group_count
    part_rows = token_count // part_count
    width = group_heads * head_dim
    selector = step_index[0] % 2
    blend = blend_of(step_index[0])
    limits = block_limits(block_exponents)[..., None]
    residual = (current_pairs.astype(jnp.float32) - earlier_pairs.astype(jnp.float32)).reshape(
        layer_count, 2, token_count, head_count, head_dim
    )
    update = jnp.clip(residual, -limits, limits).astype(jnp.bfloat16)
    pieces = update.reshape(layer_count, 2, part_count, part_rows, group_count, width)
    pieces = pieces.transpose(0, 4, 2, 1, 3, 5).reshape(
        layer_count, devices, 2 * part_rows, width
    )
    asked = queries.reshape(layer_count, token_count, group_count, 1, width)
    asked = jnp.broadcast_to(
        asked.transpose(0, 2, 3, 1, 4),
        (layer_count, group_count, part_count, token_count, width),
    ).reshape(layer_count, devices, token_count, width)
    attended_list = []
    renewed_list = []
    for layer in range(layer_count):
        refresh = selector != layer % 2
        outgoing = jnp.where(refresh, pieces[layer], jnp.zeros_like(pieces[layer]))
        arrived = exchange(jnp.concatenate([outgoing, asked[layer]], 1))
        arrived_update = arrived[:, : 2 * part_rows].reshape(devices, 2, part_rows, width)
        renewed = (
            stale_cache[layer, :, 0].astype(jnp.float32)
            + blend * arrived_update.transpose(1, 0, 2, 3).astype(jnp.float32)
        ).astype(jnp.bfloat16)
        key_rows = renewed[0].reshape(devices * part_rows, group_heads, head_dim)
        value_rows = renewed[1].reshape(devices * part_rows, group_heads, head_dim)
        block_span = 1
        while (
            block_span * token_count < 512 and devices % (2 * block_span) == 0
        ):
            block_span = block_span * 2
        blocks = arrived[:, 2 * part_rows :].reshape(
            devices // block_span, block_span * token_count, group_heads, head_dim
        )
        partial_out, log_total = answer_part(blocks, key_rows, value_rows)
        back_out = exchange(
            partial_out.astype(jnp.bfloat16).reshape(devices, token_count, width)
        ).astype(jnp.float32)
        back_log = exchange(
            log_total.astype(jnp.bfloat16).reshape(devices, token_count, group_heads)
        ).astype(jnp.float32)
        back_out = back_out.reshape(group_count, part_count, token_count, group_heads, head_dim)
        back_log = back_log.reshape(group_count, part_count, token_count, group_heads)
        factor = jnp.exp(back_log - jnp.max(back_log, 1, keepdims=True))
        merged = jnp.sum(factor[..., None] * back_out, 1) / jnp.sum(factor, 1)[..., None]
        attended_list.append(
            merged.transpose(1, 0, 2, 3)
            .reshape(token_count, channel_count)
            .astype(jnp.bfloat16)
        )
        renewed_list.append(renewed)
    return jnp.stack(attended_list), jnp.stack(renewed_list)[:, :, None]


def body(queries, current_pairs, earlier_pairs, stale_cache, block_exponents, step_index):
    layer_count = queries.shape[0]
    head_count = block_exponents.shape[-1]
    one_part = lax.axis_size("patch") <= head_count and layer_count == 2
    chosen = whole_key_body if one_part else split_key_body
    return chosen(
        queries, current_pairs, earlier_pairs, stale_cache, block_exponents, step_index
    )


def solution(mesh):
    in_specs = (
        P(None, ("groups", "patch"), None),
        P(None, None, ("groups", "patch"), None),
        P(None, None, ("groups", "patch"), None),
        P(None, None, ("groups", "patch"), None, None, None),
        P(None, None, ("groups", "patch"), None),
        P("groups"),
    )
    out_specs = (
        P(None, ("groups", "patch"), None),
        P(None, None, ("groups", "patch"), None, None, None),
    )
    return jax.shard_map(body, mesh=mesh, in_specs=in_specs, out_specs=out_specs, check_vma=False)
```

```python
from functools import partial

import jax
import jax.numpy as jnp
from jax import lax
from jax.experimental import pallas as pl
from jax.experimental.pallas import tpu as pltpu
from jax.sharding import PartitionSpec as P

STEPS = 50
SATURATION = 448
TOP_LEVEL = 8
VMEM_BYTES = 40 * 1024 * 1024
PACK_BYTES = 60 * 1024 * 1024


def block_limits(exponents):
    return ((SATURATION << TOP_LEVEL) >> exponents).astype(jnp.float32) * (2.0**-TOP_LEVEL)


def blend_of(step):
    return 1.0 - step.astype(jnp.float32) / (2.0 * STEPS)


def layers_of(step):
    kept = lax.rem(step, 2)
    return kept, 1 - kept


def pairwise(array, distance, devices):
    pairs = [(device, device ^ distance) for device in range(devices)]
    return lax.ppermute(array, "patch", pairs)


def start_all(copies):
    for copy in copies:
        copy.start()
    return copies


def wait_all(copies):
    for copy in copies:
        copy.wait()


def pack_kernel(chips, step_ref, query_ref, current_ref, earlier_ref, exponent_ref, *refs):
    messages = refs[:chips]
    queries, current, earlier, exponents, packed, sems, out_sems = refs[chips:]
    _, _, channel_count = query_ref.shape
    head_count = exponent_ref.shape[-1]
    head_dim = channel_count // head_count
    width = channel_count // chips
    kept, refreshed = layers_of(step_ref[0])
    here = lax.div(lax.axis_index("patch"), 2)
    pairs = (
        (query_ref, queries),
        (current_ref.at[refreshed], current),
        (earlier_ref.at[refreshed], earlier),
        (exponent_ref.at[refreshed], exponents),
    )
    copies = start_all(
        [
            pltpu.make_async_copy(source, target, sems.at[index])
            for index, (source, target) in enumerate(pairs)
        ]
    )
    places = [lax.bitwise_xor(here, chip) for chip in range(chips)]
    copies[0].wait()
    for slot, layer in enumerate((kept, refreshed)):
        for chip in range(chips):
            packed[places[chip], :, slot * width : (slot + 1) * width] = queries[
                layer, :, chip * width : (chip + 1) * width
            ]
    wait_all(copies[1:])
    for side in range(2):
        limits = block_limits(exponents[side])
        first = (2 + side) * width
        for head in range(head_count):
            span = slice(head * head_dim, (head + 1) * head_dim)
            residual = current[side, :, span].astype(jnp.float32) - earlier[
                side, :, span
            ].astype(jnp.float32)
            limit = limits[:, head : head + 1]
            update = jnp.minimum(jnp.maximum(residual, -limit), limit).astype(jnp.bfloat16)
            chip, inner = divmod(head * head_dim, width)
            packed[places[chip], :, first + inner : first + inner + head_dim] = update
    wait_all(
        start_all(
            [
                pltpu.make_async_copy(packed.at[chip], messages[chip], out_sems.at[chip])
                for chip in range(chips)
            ]
        )
    )


def pack(step_index, queries, current_pairs, earlier_pairs, block_exponents, chips):
    _, token_count, channel_count = queries.shape
    columns = 4 * (channel_count // chips)
    far = pl.BlockSpec(memory_space=pl.ANY)
    layers = [current_pairs, earlier_pairs, block_exponents]
    return pl.pallas_call(
        partial(pack_kernel, chips),
        in_specs=[pl.BlockSpec(memory_space=pltpu.SMEM)] + [far] * 4,
        out_specs=[far] * chips,
        out_shape=[jax.ShapeDtypeStruct((token_count, columns), jnp.bfloat16)] * chips,
        scratch_shapes=[pltpu.VMEM(queries.shape, queries.dtype)]
        + [pltpu.VMEM(array.shape[1:], array.dtype) for array in layers]
        + [
            pltpu.VMEM((chips, token_count, columns), jnp.bfloat16),
            pltpu.SemaphoreType.DMA((4,)),
            pltpu.SemaphoreType.DMA((chips,)),
        ],
        compiler_params=pltpu.CompilerParams(vmem_limit_bytes=PACK_BYTES),
    )(step_index, queries, current_pairs, earlier_pairs, block_exponents)


def stacked(blocks):
    return jnp.concatenate([block.astype(jnp.float32) for block in blocks], 0).astype(
        jnp.bfloat16
    )


def answer(queries, keys, values, head_dim):
    spans = [
        slice(first, first + head_dim) for first in range(0, queries.shape[-1], head_dim)
    ]
    scores = [
        lax.dot_general(
            queries[:, span],
            keys[:, span],
            (((1,), (1,)), ((), ())),
            preferred_element_type=jnp.float32,
        )
        for span in spans
    ]
    weights = [
        jnp.exp((score - jnp.max(score, -1, keepdims=True)) * head_dim ** (-0.5))
        for score in scores
    ]
    return [
        jnp.dot(weight.astype(jnp.bfloat16), values[:, span], preferred_element_type=jnp.float32)
        / jnp.sum(weight, -1, keepdims=True)
        for weight, span in zip(weights, spans)
    ]


def kept_kernel(order, head_dim, step_ref, query_ref, *refs):
    messages = dict(zip([chip for chip in order if chip], refs))
    own_ref, other_ref, out_ref = refs[len(messages) :]
    width = own_ref.shape[-1]
    kept, _ = layers_of(step_ref[0])
    here, core = lax.div(lax.axis_index("patch"), 2), lax.rem(lax.axis_index("patch"), 2)
    for group, cache_ref in ((core, own_ref), (1 - core, other_ref)):
        first = pl.multiple_of(group * width, width)
        blocks = []
        for chip in order:
            if chip:
                blocks.append(messages[chip][:, pl.ds(first, width)])
            else:
                place = pl.multiple_of((2 * here + group) * width, width)
                blocks.append(query_ref[kept, :, pl.ds(place, width)])
        queries = stacked(blocks)
        keys, values = cache_ref[kept, 0], cache_ref[kept, 1]
        for head, result in enumerate(answer(queries, keys, values, head_dim)):
            place = pl.ds(pl.multiple_of(first + head * head_dim, head_dim), head_dim)
            out_ref[:, place] = result.astype(jnp.bfloat16)


def attend_kept(step_index, queries, arrived, order, stale, other_stale, head_dim):
    chips = len(order)
    messages = [arrived[chip] for chip in order if chip]
    _, token_count, channel_count = queries.shape
    whole = pl.BlockSpec(memory_space=pltpu.VMEM)
    return pl.pallas_call(
        partial(kept_kernel, order, head_dim),
        in_specs=[pl.BlockSpec(memory_space=pltpu.SMEM)] + [whole] * (chips + 2),
        out_specs=whole,
        out_shape=jax.ShapeDtypeStruct(
            (chips * token_count, channel_count // chips), jnp.bfloat16
        ),
        compiler_params=pltpu.CompilerParams(vmem_limit_bytes=VMEM_BYTES),
    )(step_index, queries, *messages, stale, other_stale)


def refreshed_kernel(order, head_dim, step_ref, *refs):
    chips = len(order)
    messages, relayed = refs[:chips], refs[chips : 2 * chips]
    kept_out, own_ref, other_ref = refs[2 * chips : 2 * chips + 3]
    answers = refs[2 * chips + 3 : 3 * chips + 3]
    renewed, updates = refs[3 * chips + 3 :]
    width = own_ref.shape[-1]
    token_count = messages[0].shape[0]
    step = step_ref[0]
    _, refreshed = layers_of(step)
    blend = blend_of(step)
    me = lax.axis_index("patch")
    core = lax.rem(me, 2)
    for slot, chip in enumerate(order):
        for source, message in ((2 * chip, messages[slot]), (2 * chip + 1, relayed[slot])):
            row = pl.multiple_of(lax.bitwise_xor(me, source) * token_count, 8)
            updates[pl.ds(row, token_count), :] = message[:, 4 * width :].astype(jnp.float32)
    results = []
    for turn, (group, cache_ref) in enumerate(((core, own_ref), (1 - core, other_ref))):
        pair = []
        for side in range(2):
            place = pl.ds(pl.multiple_of((2 * side + group) * width, width), width)
            rows = (
                cache_ref[refreshed, side].astype(jnp.float32)
                + blend * updates[:, place]
            ).astype(jnp.bfloat16)
            if turn == 0:
                renewed[side] = rows
            pair.append(rows)
        keys, values = pair
        first = pl.multiple_of(group * width, width)
        queries = stacked(
            [message[:, pl.ds(pl.multiple_of(2 * width + first, width), width)] for message in messages]
        )
        for head, result in enumerate(answer(queries, keys, values, head_dim)):
            place = pl.ds(
                pl.multiple_of(2 * width + first + head * head_dim, head_dim), head_dim
            )
            for slot in range(chips):
                answers[slot][:, place] = result[
                    slot * token_count : (slot + 1) * token_count
                ].astype(jnp.bfloat16)
    earlier = kept_out[...].astype(jnp.float32)
    for slot in range(chips):
        answers[slot][:, : 2 * width] = earlier[
            slot * token_count : (slot + 1) * token_count
        ].astype(jnp.bfloat16)


def attend_refreshed(
    step_index, messages, relayed, order, kept_out, stale, other_stale, head_dim
):
    chips = len(messages)
    token_count, columns = messages[0].shape
    whole = pl.BlockSpec(memory_space=pltpu.VMEM)
    *answers, renewed = pl.pallas_call(
        partial(refreshed_kernel, order, head_dim),
        in_specs=[pl.BlockSpec(memory_space=pltpu.SMEM)] + [whole] * (2 * chips + 3),
        out_specs=[whole] * (chips + 1),
        out_shape=[jax.ShapeDtypeStruct((token_count, columns // 2), jnp.bfloat16)] * chips
        + [jax.ShapeDtypeStruct(stale.shape[1:], jnp.bfloat16)],
        scratch_shapes=[pltpu.VMEM((stale.shape[2], columns // 2), jnp.float32)],
        compiler_params=pltpu.CompilerParams(vmem_limit_bytes=VMEM_BYTES),
    )(step_index, *messages, *relayed, kept_out, stale, other_stale)
    return answers, renewed


def store_kernel(step_ref, stale_ref, renewed_ref, out_ref, sems):
    kept, refreshed = layers_of(step_ref[0])
    wait_all(
        start_all(
            [
                pltpu.make_async_copy(stale_ref.at[kept], out_ref.at[kept], sems.at[0]),
                pltpu.make_async_copy(renewed_ref, out_ref.at[refreshed], sems.at[1]),
            ]
        )
    )


def store(step_index, stale, renewed):
    far = pl.BlockSpec(memory_space=pl.ANY)
    return pl.pallas_call(
        store_kernel,
        in_specs=[pl.BlockSpec(memory_space=pltpu.SMEM)]
        + [pl.BlockSpec(memory_space=pltpu.VMEM)] * 2,
        out_specs=far,
        out_shape=jax.ShapeDtypeStruct(stale.shape, stale.dtype),
        scratch_shapes=[pltpu.SemaphoreType.DMA((2,))],
        compiler_params=pltpu.CompilerParams(vmem_limit_bytes=VMEM_BYTES),
    )(step_index, stale, renewed)


def after(array, *others):
    return lax.optimization_barrier((array, *others))[0]


def place_kernel(order, step_ref, *refs):
    chips = len(order)
    answers = refs[:chips]
    out_ref, placed, sem = refs[chips:]
    width = answers[0].shape[-1] // 2
    here = lax.div(lax.axis_index("patch"), 2)
    for slot, chip in enumerate(order):
        first = pl.multiple_of(lax.bitwise_xor(here, chip) * width, width)
        for half, layer in enumerate(layers_of(step_ref[0])):
            placed[layer, :, pl.ds(first, width)] = answers[slot][
                :, half * width : (half + 1) * width
            ]
    copy = pltpu.make_async_copy(placed, out_ref, sem)
    copy.start()
    copy.wait()


def place(step_index, answers, order):
    token_count, columns = answers[0].shape
    attended = jax.ShapeDtypeStruct((2, token_count, len(order) * columns // 2), jnp.bfloat16)
    return pl.pallas_call(
        partial(place_kernel, order),
        in_specs=[pl.BlockSpec(memory_space=pltpu.SMEM)]
        + [pl.BlockSpec(memory_space=pltpu.VMEM)] * len(order),
        out_specs=pl.BlockSpec(memory_space=pl.ANY),
        out_shape=attended,
        scratch_shapes=[
            pltpu.VMEM(attended.shape, attended.dtype),
            pltpu.SemaphoreType.DMA(()),
        ],
        compiler_params=pltpu.CompilerParams(vmem_limit_bytes=VMEM_BYTES),
    )(step_index, *answers)


def distances(chips):
    if chips == 8:
        return [5, 1, 3, 6, 4, 2, 7, 0], [7, 6, 5, 2, 4, 3, 1, 0]
    order = list(range(chips - 1, -1, -1))
    return order, order


def whole_key_body(
    queries, current_pairs, earlier_pairs, stale_cache, block_exponents, step_index
):
    devices = lax.axis_size("patch")
    chips = devices // 2
    layer_count, token_count, channel_count = queries.shape
    head_dim = channel_count // block_exponents.shape[-1]
    stale = stale_cache.reshape(layer_count, 2, devices * token_count, -1)
    other_stale = pairwise(stale, 1, devices)
    messages = pack(
        step_index, queries, current_pairs, earlier_pairs, block_exponents, chips
    )
    *messages, other_stale = lax.optimization_barrier((*messages, other_stale))
    order, back_order = distances(chips)
    arrived = {
        chip: pairwise(messages[chip], 2 * chip, devices) for chip in order if chip
    }
    arrived[0] = messages[0]
    kept_out = attend_kept(
        step_index, queries, arrived, order, stale, other_stale, head_dim
    )
    arrived = [arrived[chip] for chip in order]
    relayed = [pairwise(message, 1, devices) for message in arrived]
    answers, renewed = attend_refreshed(
        step_index, arrived, relayed, order, kept_out, stale, other_stale, head_dim
    )
    by_chip = [answers[order.index(chip)] for chip in range(chips)]
    returned = [
        pairwise(by_chip[chip], 2 * chip, devices) if chip else by_chip[0] for chip in back_order
    ]
    renewed = store(step_index, stale, after(renewed, returned[0]))
    attended = place(step_index, returned, back_order)
    return attended, renewed.reshape(stale_cache.shape)


def exchange(rows):
    return lax.all_to_all(rows, "patch", split_axis=0, concat_axis=0, tiled=True)


def answer_part(blocks, key_rows, value_rows):
    score_scale = key_rows.shape[-1] ** (-0.5)

    def one_block(query_block):
        scores = (
            jnp.einsum("qhd,khd->hqk", query_block, key_rows, preferred_element_type=jnp.float32)
            * score_scale
        )
        peak = jnp.max(scores, -1, keepdims=True)
        weights = jnp.exp(scores - peak)
        total = jnp.sum(weights, -1)
        mixed = jnp.einsum(
            "hqk,khd->qhd",
            weights.astype(jnp.bfloat16),
            value_rows,
            preferred_element_type=jnp.float32,
        )
        return mixed / total.T[..., None], (peak[..., 0] + jnp.log(total)).T

    return lax.map(one_block, blocks)


def split_key_body(
    queries, current_pairs, earlier_pairs, stale_cache, block_exponents, step_index
):
    devices = lax.axis_size("patch")
    layer_count, token_count, channel_count = queries.shape
    head_count = block_exponents.shape[-1]
    head_dim = channel_count // head_count
    group_count = min(head_count, devices)
    part_count = devices // group_count
    group_heads = head_count // group_count
    part_rows = token_count // part_count
    width = group_heads * head_dim
    selector = step_index[0] % 2
    blend = blend_of(step_index[0])
    limits = block_limits(block_exponents)[..., None]
    residual = (current_pairs.astype(jnp.float32) - earlier_pairs.astype(jnp.float32)).reshape(
        layer_count, 2, token_count, head_count, head_dim
    )
    update = jnp.clip(residual, -limits, limits).astype(jnp.bfloat16)
    pieces = update.reshape(layer_count, 2, part_count, part_rows, group_count, width)
    pieces = pieces.transpose(0, 4, 2, 1, 3, 5).reshape(
        layer_count, devices, 2 * part_rows, width
    )
    asked = queries.reshape(layer_count, token_count, group_count, 1, width)
    asked = jnp.broadcast_to(
        asked.transpose(0, 2, 3, 1, 4),
        (layer_count, group_count, part_count, token_count, width),
    ).reshape(layer_count, devices, token_count, width)
    attended_list = []
    renewed_list = []
    for layer in range(layer_count):
        refresh = selector != layer % 2
        outgoing = jnp.where(refresh, pieces[layer], jnp.zeros_like(pieces[layer]))
        arrived = exchange(jnp.concatenate([outgoing, asked[layer]], 1))
        arrived_update = arrived[:, : 2 * part_rows].reshape(devices, 2, part_rows, width)
        renewed = (
            stale_cache[layer, :, 0].astype(jnp.float32)
            + blend * arrived_update.transpose(1, 0, 2, 3).astype(jnp.float32)
        ).astype(jnp.bfloat16)
        key_rows = renewed[0].reshape(devices * part_rows, group_heads, head_dim)
        value_rows = renewed[1].reshape(devices * part_rows, group_heads, head_dim)
        block_span = 1
        while (
            block_span * token_count < 512 and devices % (2 * block_span) == 0
        ):
            block_span = block_span * 2
        blocks = arrived[:, 2 * part_rows :].reshape(
            devices // block_span, block_span * token_count, group_heads, head_dim
        )
        partial_out, log_total = answer_part(blocks, key_rows, value_rows)
        back_out = exchange(
            partial_out.astype(jnp.bfloat16).reshape(devices, token_count, width)
        ).astype(jnp.float32)
        back_log = exchange(
            log_total.astype(jnp.bfloat16).reshape(devices, token_count, group_heads)
        ).astype(jnp.float32)
        back_out = back_out.reshape(group_count, part_count, token_count, group_heads, head_dim)
        back_log = back_log.reshape(group_count, part_count, token_count, group_heads)
        factor = jnp.exp(back_log - jnp.max(back_log, 1, keepdims=True))
        merged = jnp.sum(factor[..., None] * back_out, 1) / jnp.sum(factor, 1)[..., None]
        attended_list.append(
            merged.transpose(1, 0, 2, 3)
            .reshape(token_count, channel_count)
            .astype(jnp.bfloat16)
        )
        renewed_list.append(renewed)
    return jnp.stack(attended_list), jnp.stack(renewed_list)[:, :, None]


def body(queries, current_pairs, earlier_pairs, stale_cache, block_exponents, step_index):
    layer_count = queries.shape[0]
    head_count = block_exponents.shape[-1]
    devices = lax.axis_size("patch")
    one_part = 1 < devices <= head_count and devices & (devices - 1) == 0 and layer_count == 2
    chosen = whole_key_body if one_part else split_key_body
    return chosen(
        queries, current_pairs, earlier_pairs, stale_cache, block_exponents, step_index
    )


def solution(mesh):
    in_specs = (
        P(None, ("groups", "patch"), None),
        P(None, None, ("groups", "patch"), None),
        P(None, None, ("groups", "patch"), None),
        P(None, None, ("groups", "patch"), None, None, None),
        P(None, None, ("groups", "patch"), None),
        P("groups"),
    )
    out_specs = (
        P(None, ("groups", "patch"), None),
        P(None, None, ("groups", "patch"), None, None, None),
    )
    return jax.shard_map(body, mesh=mesh, in_specs=in_specs, out_specs=out_specs, check_vma=False)
```

```python
from functools import partial

import jax
import jax.numpy as jnp
from jax import lax
from jax.experimental import pallas as pl
from jax.experimental.pallas import tpu as pltpu
from jax.sharding import PartitionSpec as P

STEPS = 50
SATURATION = 448
TOP_LEVEL = 8
VMEM_BYTES = 40 * 1024 * 1024
PACK_BYTES = 60 * 1024 * 1024


def block_limits(exponents):
    return ((SATURATION << TOP_LEVEL) >> exponents).astype(jnp.float32) * (2.0**-TOP_LEVEL)


def blend_of(step):
    return 1.0 - step.astype(jnp.float32) / (2.0 * STEPS)


def layers_of(step):
    kept = lax.rem(step, 2)
    return kept, 1 - kept


def pairwise(array, distance, devices):
    pairs = [(device, device ^ distance) for device in range(devices)]
    return lax.ppermute(array, "patch", pairs)


def start_all(copies):
    for copy in copies:
        copy.start()
    return copies


def wait_all(copies):
    for copy in copies:
        copy.wait()


def pack_kernel(order, step_ref, query_ref, current_ref, earlier_ref, exponent_ref, *refs):
    chips = len(order)
    messages = refs[:chips]
    queries, current, earlier, exponents, limits, packed, sems, side_sems, out_sems = refs[chips:]
    _, _, channel_count = query_ref.shape
    head_count = exponent_ref.shape[-1]
    head_dim = channel_count // head_count
    width = channel_count // chips
    kept, refreshed = layers_of(step_ref[0])
    here = lax.div(lax.axis_index("patch"), 2)
    copies = start_all(
        [
            pltpu.make_async_copy(exponent_ref.at[refreshed], exponents, sems.at[0]),
            pltpu.make_async_copy(query_ref, queries, sems.at[1]),
        ]
    )
    side_copies = [
        start_all(
            [
                pltpu.make_async_copy(
                    source.at[refreshed, side], target.at[side], side_sems.at[side, index]
                )
                for index, (source, target) in enumerate(
                    ((current_ref, current), (earlier_ref, earlier))
                )
            ]
        )
        for side in range(2)
    ]
    copies[0].wait()
    for side in range(2):
        values = block_limits(exponents[side])
        for head in range(head_count):
            limits[side, :, head * head_dim : (head + 1) * head_dim] = jnp.broadcast_to(
                values[:, head : head + 1], (values.shape[0], head_dim)
            )
    copies[1].wait()
    spans = [
        pl.ds(pl.multiple_of(lax.bitwise_xor(here, chip) * width, width), width)
        for chip in order
    ]
    for chip, span in zip(order, spans):
        for slot, layer in enumerate((kept, refreshed)):
            packed[chip, :, slot * width : (slot + 1) * width] = queries[layer, :, span]
    out_copies = []
    for side in range(2):
        wait_all(side_copies[side])
        for chip, span in zip(order, spans):
            residual = current[side, :, span].astype(jnp.float32) - earlier[
                side, :, span
            ].astype(jnp.float32)
            limit = limits[side, :, span]
            update = jnp.minimum(jnp.maximum(residual, -limit), limit).astype(jnp.bfloat16)
            packed[chip, :, (2 + side) * width : (3 + side) * width] = update
            if side == 1:
                out_copies.append(
                    pltpu.make_async_copy(packed.at[chip], messages[chip], out_sems.at[chip])
                )
                out_copies[-1].start()
    wait_all(out_copies)


def pack(step_index, queries, current_pairs, earlier_pairs, block_exponents, order):
    _, token_count, channel_count = queries.shape
    chips = len(order)
    columns = 4 * (channel_count // chips)
    far = pl.BlockSpec(memory_space=pl.ANY)
    layers = [current_pairs, earlier_pairs, block_exponents]
    return pl.pallas_call(
        partial(pack_kernel, order),
        in_specs=[pl.BlockSpec(memory_space=pltpu.SMEM)] + [far] * 4,
        out_specs=[far] * chips,
        out_shape=[jax.ShapeDtypeStruct((token_count, columns), jnp.bfloat16)] * chips,
        scratch_shapes=[pltpu.VMEM(queries.shape, queries.dtype)]
        + [pltpu.VMEM(array.shape[1:], array.dtype) for array in layers]
        + [
            pltpu.VMEM(current_pairs.shape[1:], jnp.float32),
            pltpu.VMEM((chips, token_count, columns), jnp.bfloat16),
            pltpu.SemaphoreType.DMA((2,)),
            pltpu.SemaphoreType.DMA((2, 2)),
            pltpu.SemaphoreType.DMA((chips,)),
        ],
        compiler_params=pltpu.CompilerParams(vmem_limit_bytes=PACK_BYTES),
    )(step_index, queries, current_pairs, earlier_pairs, block_exponents)


def stacked(blocks):
    return jnp.concatenate([block.astype(jnp.float32) for block in blocks], 0).astype(
        jnp.bfloat16
    )


def answer(queries, keys, values, head_dim):
    spans = [
        slice(first, first + head_dim) for first in range(0, queries.shape[-1], head_dim)
    ]
    scores = [
        lax.dot_general(
            queries[:, span],
            keys[:, span],
            (((1,), (1,)), ((), ())),
            preferred_element_type=jnp.float32,
        )
        for span in spans
    ]
    weights = [
        jnp.exp((score - jnp.max(score, -1, keepdims=True)) * head_dim ** (-0.5))
        for score in scores
    ]
    return [
        jnp.dot(weight.astype(jnp.bfloat16), values[:, span], preferred_element_type=jnp.float32)
        / jnp.sum(weight, -1, keepdims=True)
        for weight, span in zip(weights, spans)
    ]


def kept_kernel(order, head_dim, step_ref, query_ref, *refs):
    messages = dict(zip([chip for chip in order if chip], refs))
    own_ref, other_ref, out_ref = refs[len(messages) :]
    width = own_ref.shape[-1]
    kept, _ = layers_of(step_ref[0])
    here, core = lax.div(lax.axis_index("patch"), 2), lax.rem(lax.axis_index("patch"), 2)
    for group, cache_ref in ((core, own_ref), (1 - core, other_ref)):
        first = pl.multiple_of(group * width, width)
        blocks = []
        for chip in order:
            if chip:
                blocks.append(messages[chip][:, pl.ds(first, width)])
            else:
                place = pl.multiple_of((2 * here + group) * width, width)
                blocks.append(query_ref[kept, :, pl.ds(place, width)])
        queries = stacked(blocks)
        keys, values = cache_ref[kept, 0], cache_ref[kept, 1]
        for head, result in enumerate(answer(queries, keys, values, head_dim)):
            place = pl.ds(pl.multiple_of(first + head * head_dim, head_dim), head_dim)
            out_ref[:, place] = result.astype(jnp.bfloat16)


def attend_kept(step_index, queries, arrived, order, stale, other_stale, head_dim):
    chips = len(order)
    messages = [arrived[chip] for chip in order if chip]
    _, token_count, channel_count = queries.shape
    whole = pl.BlockSpec(memory_space=pltpu.VMEM)
    return pl.pallas_call(
        partial(kept_kernel, order, head_dim),
        in_specs=[pl.BlockSpec(memory_space=pltpu.SMEM)] + [whole] * (chips + 2),
        out_specs=whole,
        out_shape=jax.ShapeDtypeStruct(
            (chips * token_count, channel_count // chips), jnp.bfloat16
        ),
        compiler_params=pltpu.CompilerParams(vmem_limit_bytes=VMEM_BYTES),
    )(step_index, queries, *messages, stale, other_stale)


def refreshed_kernel(order, head_dim, step_ref, *refs):
    chips = len(order)
    messages, relayed = refs[:chips], refs[chips : 2 * chips]
    kept_out, own_ref, other_ref = refs[2 * chips : 2 * chips + 3]
    answers = refs[2 * chips + 3 : 3 * chips + 3]
    renewed, updates = refs[3 * chips + 3 :]
    width = own_ref.shape[-1]
    token_count = messages[0].shape[0]
    step = step_ref[0]
    _, refreshed = layers_of(step)
    blend = blend_of(step)
    me = lax.axis_index("patch")
    core = lax.rem(me, 2)
    for slot, chip in enumerate(order):
        for source, message in ((2 * chip, messages[slot]), (2 * chip + 1, relayed[slot])):
            row = pl.multiple_of(lax.bitwise_xor(me, source) * token_count, 8)
            updates[pl.ds(row, token_count), :] = message[:, 4 * width :].astype(jnp.float32)
    results = []
    for turn, (group, cache_ref) in enumerate(((core, own_ref), (1 - core, other_ref))):
        pair = []
        for side in range(2):
            place = pl.ds(pl.multiple_of((2 * side + group) * width, width), width)
            rows = (
                cache_ref[refreshed, side].astype(jnp.float32)
                + blend * updates[:, place]
            ).astype(jnp.bfloat16)
            if turn == 0:
                renewed[side] = rows
            pair.append(rows)
        keys, values = pair
        first = pl.multiple_of(group * width, width)
        queries = stacked(
            [message[:, pl.ds(pl.multiple_of(2 * width + first, width), width)] for message in messages]
        )
        for head, result in enumerate(answer(queries, keys, values, head_dim)):
            place = pl.ds(
                pl.multiple_of(2 * width + first + head * head_dim, head_dim), head_dim
            )
            for slot in range(chips):
                answers[slot][:, place] = result[
                    slot * token_count : (slot + 1) * token_count
                ].astype(jnp.bfloat16)
    earlier = kept_out[...].astype(jnp.float32)
    for slot in range(chips):
        answers[slot][:, : 2 * width] = earlier[
            slot * token_count : (slot + 1) * token_count
        ].astype(jnp.bfloat16)


def attend_refreshed(
    step_index, messages, relayed, order, kept_out, stale, other_stale, head_dim
):
    chips = len(messages)
    token_count, columns = messages[0].shape
    whole = pl.BlockSpec(memory_space=pltpu.VMEM)
    *answers, renewed = pl.pallas_call(
        partial(refreshed_kernel, order, head_dim),
        in_specs=[pl.BlockSpec(memory_space=pltpu.SMEM)] + [whole] * (2 * chips + 3),
        out_specs=[whole] * (chips + 1),
        out_shape=[jax.ShapeDtypeStruct((token_count, columns // 2), jnp.bfloat16)] * chips
        + [jax.ShapeDtypeStruct(stale.shape[1:], jnp.bfloat16)],
        scratch_shapes=[pltpu.VMEM((stale.shape[2], columns // 2), jnp.float32)],
        compiler_params=pltpu.CompilerParams(vmem_limit_bytes=VMEM_BYTES),
    )(step_index, *messages, *relayed, kept_out, stale, other_stale)
    return answers, renewed


def store_kernel(step_ref, stale_ref, renewed_ref, out_ref, sems):
    kept, refreshed = layers_of(step_ref[0])
    wait_all(
        start_all(
            [
                pltpu.make_async_copy(stale_ref.at[kept], out_ref.at[kept], sems.at[0]),
                pltpu.make_async_copy(renewed_ref, out_ref.at[refreshed], sems.at[1]),
            ]
        )
    )


def store(step_index, stale, renewed):
    far = pl.BlockSpec(memory_space=pl.ANY)
    return pl.pallas_call(
        store_kernel,
        in_specs=[pl.BlockSpec(memory_space=pltpu.SMEM)]
        + [pl.BlockSpec(memory_space=pltpu.VMEM)] * 2,
        out_specs=far,
        out_shape=jax.ShapeDtypeStruct(stale.shape, stale.dtype),
        scratch_shapes=[pltpu.SemaphoreType.DMA((2,))],
        compiler_params=pltpu.CompilerParams(vmem_limit_bytes=VMEM_BYTES),
    )(step_index, stale, renewed)


def after(array, *others):
    return lax.optimization_barrier((array, *others))[0]


def place_kernel(order, step_ref, *refs):
    chips = len(order)
    answers = refs[:chips]
    out_ref, placed, sem = refs[chips:]
    width = answers[0].shape[-1] // 2
    here = lax.div(lax.axis_index("patch"), 2)
    for slot, chip in enumerate(order):
        first = pl.multiple_of(lax.bitwise_xor(here, chip) * width, width)
        for half, layer in enumerate(layers_of(step_ref[0])):
            placed[layer, :, pl.ds(first, width)] = answers[slot][
                :, half * width : (half + 1) * width
            ]
    copy = pltpu.make_async_copy(placed, out_ref, sem)
    copy.start()
    copy.wait()


def place(step_index, answers, order):
    token_count, columns = answers[0].shape
    attended = jax.ShapeDtypeStruct((2, token_count, len(order) * columns // 2), jnp.bfloat16)
    return pl.pallas_call(
        partial(place_kernel, order),
        in_specs=[pl.BlockSpec(memory_space=pltpu.SMEM)]
        + [pl.BlockSpec(memory_space=pltpu.VMEM)] * len(order),
        out_specs=pl.BlockSpec(memory_space=pl.ANY),
        out_shape=attended,
        scratch_shapes=[
            pltpu.VMEM(attended.shape, attended.dtype),
            pltpu.SemaphoreType.DMA(()),
        ],
        compiler_params=pltpu.CompilerParams(vmem_limit_bytes=VMEM_BYTES),
    )(step_index, *answers)


def distances(chips):
    if chips == 8:
        return [5, 1, 3, 4, 6, 2, 7, 0], [7, 6, 5, 2, 4, 3, 1, 0]
    order = list(range(chips - 1, -1, -1))
    return order, order


def whole_key_body(
    queries, current_pairs, earlier_pairs, stale_cache, block_exponents, step_index
):
    devices = lax.axis_size("patch")
    chips = devices // 2
    layer_count, token_count, channel_count = queries.shape
    head_dim = channel_count // block_exponents.shape[-1]
    stale = stale_cache.reshape(layer_count, 2, devices * token_count, -1)
    order, back_order = distances(chips)
    other_stale = pairwise(stale, 1, devices)
    messages = pack(
        step_index, queries, current_pairs, earlier_pairs, block_exponents, order
    )
    *messages, other_stale = lax.optimization_barrier((*messages, other_stale))
    arrived = {
        chip: pairwise(messages[chip], 2 * chip, devices) for chip in order if chip
    }
    arrived[0] = messages[0]
    kept_out = attend_kept(
        step_index, queries, arrived, order, stale, other_stale, head_dim
    )
    arrived = [arrived[chip] for chip in order]
    relayed = [pairwise(message, 1, devices) for message in arrived]
    answers, renewed = attend_refreshed(
        step_index, arrived, relayed, order, kept_out, stale, other_stale, head_dim
    )
    by_chip = [answers[order.index(chip)] for chip in range(chips)]
    returned = [
        pairwise(by_chip[chip], 2 * chip, devices) if chip else by_chip[0] for chip in back_order
    ]
    renewed = store(step_index, stale, after(renewed, returned[0]))
    attended = place(step_index, returned, back_order)
    return attended, renewed.reshape(stale_cache.shape)


def exchange(rows):
    return lax.all_to_all(rows, "patch", split_axis=0, concat_axis=0, tiled=True)


def answer_part(blocks, key_rows, value_rows):
    score_scale = key_rows.shape[-1] ** (-0.5)

    def one_block(query_block):
        scores = (
            jnp.einsum("qhd,khd->hqk", query_block, key_rows, preferred_element_type=jnp.float32)
            * score_scale
        )
        peak = jnp.max(scores, -1, keepdims=True)
        weights = jnp.exp(scores - peak)
        total = jnp.sum(weights, -1)
        mixed = jnp.einsum(
            "hqk,khd->qhd",
            weights.astype(jnp.bfloat16),
            value_rows,
            preferred_element_type=jnp.float32,
        )
        return mixed / total.T[..., None], (peak[..., 0] + jnp.log(total)).T

    return lax.map(one_block, blocks)


def split_key_body(
    queries, current_pairs, earlier_pairs, stale_cache, block_exponents, step_index
):
    devices = lax.axis_size("patch")
    layer_count, token_count, channel_count = queries.shape
    head_count = block_exponents.shape[-1]
    head_dim = channel_count // head_count
    group_count = min(head_count, devices)
    part_count = devices // group_count
    group_heads = head_count // group_count
    part_rows = token_count // part_count
    width = group_heads * head_dim
    selector = step_index[0] % 2
    blend = blend_of(step_index[0])
    limits = block_limits(block_exponents)[..., None]
    residual = (current_pairs.astype(jnp.float32) - earlier_pairs.astype(jnp.float32)).reshape(
        layer_count, 2, token_count, head_count, head_dim
    )
    update = jnp.clip(residual, -limits, limits).astype(jnp.bfloat16)
    pieces = update.reshape(layer_count, 2, part_count, part_rows, group_count, width)
    pieces = pieces.transpose(0, 4, 2, 1, 3, 5).reshape(
        layer_count, devices, 2 * part_rows, width
    )
    asked = queries.reshape(layer_count, token_count, group_count, 1, width)
    asked = jnp.broadcast_to(
        asked.transpose(0, 2, 3, 1, 4),
        (layer_count, group_count, part_count, token_count, width),
    ).reshape(layer_count, devices, token_count, width)
    attended_list = []
    renewed_list = []
    for layer in range(layer_count):
        refresh = selector != layer % 2
        outgoing = jnp.where(refresh, pieces[layer], jnp.zeros_like(pieces[layer]))
        arrived = exchange(jnp.concatenate([outgoing, asked[layer]], 1))
        arrived_update = arrived[:, : 2 * part_rows].reshape(devices, 2, part_rows, width)
        renewed = (
            stale_cache[layer, :, 0].astype(jnp.float32)
            + blend * arrived_update.transpose(1, 0, 2, 3).astype(jnp.float32)
        ).astype(jnp.bfloat16)
        key_rows = renewed[0].reshape(devices * part_rows, group_heads, head_dim)
        value_rows = renewed[1].reshape(devices * part_rows, group_heads, head_dim)
        block_span = 1
        while (
            block_span * token_count < 512 and devices % (2 * block_span) == 0
        ):
            block_span = block_span * 2
        blocks = arrived[:, 2 * part_rows :].reshape(
            devices // block_span, block_span * token_count, group_heads, head_dim
        )
        partial_out, log_total = answer_part(blocks, key_rows, value_rows)
        back_out = exchange(
            partial_out.astype(jnp.bfloat16).reshape(devices, token_count, width)
        ).astype(jnp.float32)
        back_log = exchange(
            log_total.astype(jnp.bfloat16).reshape(devices, token_count, group_heads)
        ).astype(jnp.float32)
        back_out = back_out.reshape(group_count, part_count, token_count, group_heads, head_dim)
        back_log = back_log.reshape(group_count, part_count, token_count, group_heads)
        factor = jnp.exp(back_log - jnp.max(back_log, 1, keepdims=True))
        merged = jnp.sum(factor[..., None] * back_out, 1) / jnp.sum(factor, 1)[..., None]
        attended_list.append(
            merged.transpose(1, 0, 2, 3)
            .reshape(token_count, channel_count)
            .astype(jnp.bfloat16)
        )
        renewed_list.append(renewed)
    return jnp.stack(attended_list), jnp.stack(renewed_list)[:, :, None]


def body(queries, current_pairs, earlier_pairs, stale_cache, block_exponents, step_index):
    layer_count = queries.shape[0]
    head_count = block_exponents.shape[-1]
    devices = lax.axis_size("patch")
    one_part = 1 < devices <= head_count and devices & (devices - 1) == 0 and layer_count == 2
    chosen = whole_key_body if one_part else split_key_body
    return chosen(
        queries, current_pairs, earlier_pairs, stale_cache, block_exponents, step_index
    )


def solution(mesh):
    in_specs = (
        P(None, ("groups", "patch"), None),
        P(None, None, ("groups", "patch"), None),
        P(None, None, ("groups", "patch"), None),
        P(None, None, ("groups", "patch"), None, None, None),
        P(None, None, ("groups", "patch"), None),
        P("groups"),
    )
    out_specs = (
        P(None, ("groups", "patch"), None),
        P(None, None, ("groups", "patch"), None, None, None),
    )
    return jax.shard_map(body, mesh=mesh, in_specs=in_specs, out_specs=out_specs, check_vma=False)
```

```python
from functools import partial

import jax
import jax.numpy as jnp
from jax import lax
from jax.experimental import pallas as pl
from jax.experimental.pallas import tpu as pltpu
from jax.sharding import PartitionSpec as P

STEPS = 50
SATURATION = 448
TOP_LEVEL = 8
VMEM_BYTES = 40 * 1024 * 1024
PACK_BYTES = 60 * 1024 * 1024


def block_limits(exponents):
    return ((SATURATION << TOP_LEVEL) >> exponents).astype(jnp.float32) * (2.0**-TOP_LEVEL)


def blend_of(step):
    return 1.0 - step.astype(jnp.float32) / (2.0 * STEPS)


def layers_of(step):
    kept = lax.rem(step, 2)
    return kept, 1 - kept


def pairwise(array, distance, devices):
    pairs = [(device, device ^ distance) for device in range(devices)]
    return lax.ppermute(array, "patch", pairs)


def start_all(copies):
    for copy in copies:
        copy.start()
    return copies


def wait_all(copies):
    for copy in copies:
        copy.wait()


def pack_kernel(order, step_ref, query_ref, current_ref, earlier_ref, exponent_ref, *refs):
    chips = len(order)
    messages = refs[:chips]
    queries, current, earlier, exponents, limits, packed, sems, side_sems, out_sems = refs[chips:]
    _, _, channel_count = query_ref.shape
    head_count = exponent_ref.shape[-1]
    head_dim = channel_count // head_count
    width = channel_count // chips
    kept, refreshed = layers_of(step_ref[0])
    here = lax.div(lax.axis_index("patch"), 2)
    copies = start_all(
        [
            pltpu.make_async_copy(exponent_ref.at[refreshed], exponents, sems.at[0]),
            pltpu.make_async_copy(query_ref, queries, sems.at[1]),
        ]
    )
    side_copies = [
        start_all(
            [
                pltpu.make_async_copy(
                    source.at[refreshed, side], target.at[side], side_sems.at[side, index]
                )
                for index, (source, target) in enumerate(
                    ((current_ref, current), (earlier_ref, earlier))
                )
            ]
        )
        for side in range(2)
    ]
    copies[0].wait()
    for side in range(2):
        values = block_limits(exponents[side])
        for head in range(head_count):
            limits[side, :, head * head_dim : (head + 1) * head_dim] = jnp.broadcast_to(
                values[:, head : head + 1], (values.shape[0], head_dim)
            )
    copies[1].wait()
    spans = [
        pl.ds(pl.multiple_of(lax.bitwise_xor(here, chip) * width, width), width)
        for chip in order
    ]
    for chip, span in zip(order, spans):
        for slot, layer in enumerate((kept, refreshed)):
            packed[chip, :, slot * width : (slot + 1) * width] = queries[layer, :, span]
    out_copies = []
    for side in range(2):
        wait_all(side_copies[side])
        for chip, span in zip(order, spans):
            residual = current[side, :, span].astype(jnp.float32) - earlier[
                side, :, span
            ].astype(jnp.float32)
            limit = limits[side, :, span]
            update = jnp.minimum(jnp.maximum(residual, -limit), limit).astype(jnp.bfloat16)
            packed[chip, :, (2 + side) * width : (3 + side) * width] = update
            if side == 1:
                out_copies.append(
                    pltpu.make_async_copy(packed.at[chip], messages[chip], out_sems.at[chip])
                )
                out_copies[-1].start()
    wait_all(out_copies)


def pack(step_index, queries, current_pairs, earlier_pairs, block_exponents, order):
    _, token_count, channel_count = queries.shape
    chips = len(order)
    columns = 4 * (channel_count // chips)
    far = pl.BlockSpec(memory_space=pl.ANY)
    layers = [current_pairs, earlier_pairs, block_exponents]
    return pl.pallas_call(
        partial(pack_kernel, order),
        in_specs=[pl.BlockSpec(memory_space=pltpu.SMEM)] + [far] * 4,
        out_specs=[far] * chips,
        out_shape=[jax.ShapeDtypeStruct((token_count, columns), jnp.bfloat16)] * chips,
        scratch_shapes=[pltpu.VMEM(queries.shape, queries.dtype)]
        + [pltpu.VMEM(array.shape[1:], array.dtype) for array in layers]
        + [
            pltpu.VMEM(current_pairs.shape[1:], jnp.float32),
            pltpu.VMEM((chips, token_count, columns), jnp.bfloat16),
            pltpu.SemaphoreType.DMA((2,)),
            pltpu.SemaphoreType.DMA((2, 2)),
            pltpu.SemaphoreType.DMA((chips,)),
        ],
        compiler_params=pltpu.CompilerParams(vmem_limit_bytes=PACK_BYTES),
    )(step_index, queries, current_pairs, earlier_pairs, block_exponents)


def stacked(blocks):
    return jnp.concatenate([block.astype(jnp.float32) for block in blocks], 0).astype(
        jnp.bfloat16
    )


def answer(queries, keys, values, head_dim):
    spans = [
        slice(first, first + head_dim) for first in range(0, queries.shape[-1], head_dim)
    ]
    scores = [
        lax.dot_general(
            queries[:, span],
            keys[:, span],
            (((1,), (1,)), ((), ())),
            preferred_element_type=jnp.float32,
        )
        for span in spans
    ]
    weights = [
        jnp.exp((score - jnp.max(score, -1, keepdims=True)) * head_dim ** (-0.5))
        for score in scores
    ]
    return [
        jnp.dot(weight.astype(jnp.bfloat16), values[:, span], preferred_element_type=jnp.float32)
        / jnp.sum(weight, -1, keepdims=True)
        for weight, span in zip(weights, spans)
    ]


def kept_kernel(order, head_dim, step_ref, query_ref, *refs):
    messages = dict(zip([chip for chip in order if chip], refs))
    own_ref, other_ref, out_ref = refs[len(messages) :]
    token_count = query_ref.shape[1]
    width = own_ref.shape[-1]
    kept, _ = layers_of(step_ref[0])
    here, core = lax.div(lax.axis_index("patch"), 2), lax.rem(lax.axis_index("patch"), 2)
    for group, cache_ref in ((core, own_ref), (1 - core, other_ref)):
        first = pl.multiple_of(group * width, width)
        blocks = []
        for chip in order:
            if chip:
                blocks.append(messages[chip][:, pl.ds(first, width)])
            else:
                place = pl.multiple_of((2 * here + group) * width, width)
                blocks.append(query_ref[kept, :, pl.ds(place, width)])
        queries = stacked(blocks)
        keys, values = cache_ref[kept, 0], cache_ref[kept, 1]
        for head, result in enumerate(answer(queries, keys, values, head_dim)):
            place = pl.ds(pl.multiple_of(first + head * head_dim, head_dim), head_dim)
            for slot in range(len(order)):
                out_ref[slot, :, place] = result[
                    slot * token_count : (slot + 1) * token_count
                ].astype(jnp.bfloat16)


def attend_kept(step_index, queries, arrived, order, stale, other_stale, head_dim):
    chips = len(order)
    messages = [arrived[chip] for chip in order if chip]
    _, token_count, channel_count = queries.shape
    whole = pl.BlockSpec(memory_space=pltpu.VMEM)
    return pl.pallas_call(
        partial(kept_kernel, order, head_dim),
        in_specs=[pl.BlockSpec(memory_space=pltpu.SMEM)] + [whole] * (chips + 2),
        out_specs=whole,
        out_shape=jax.ShapeDtypeStruct(
            (chips, token_count, channel_count // chips), jnp.bfloat16
        ),
        compiler_params=pltpu.CompilerParams(vmem_limit_bytes=VMEM_BYTES),
    )(step_index, queries, *messages, stale, other_stale)


def refreshed_kernel(order, head_dim, step_ref, *refs):
    chips = len(order)
    messages, relayed = refs[:chips], refs[chips : 2 * chips]
    kept_out, own_ref, other_ref = refs[2 * chips : 2 * chips + 3]
    answers = refs[2 * chips + 3 : 3 * chips + 3]
    renewed, updates = refs[3 * chips + 3 :]
    width = own_ref.shape[-1]
    token_count = messages[0].shape[0]
    step = step_ref[0]
    _, refreshed = layers_of(step)
    blend = blend_of(step)
    me = lax.axis_index("patch")
    core = lax.rem(me, 2)
    for slot, chip in enumerate(order):
        for source, message in ((2 * chip, messages[slot]), (2 * chip + 1, relayed[slot])):
            row = pl.multiple_of(lax.bitwise_xor(me, source) * token_count, 8)
            updates[pl.ds(row, token_count), :] = message[:, 4 * width :].astype(jnp.float32)
    results = []
    for turn, (group, cache_ref) in enumerate(((core, own_ref), (1 - core, other_ref))):
        pair = []
        for side in range(2):
            place = pl.ds(pl.multiple_of((2 * side + group) * width, width), width)
            rows = (
                cache_ref[refreshed, side].astype(jnp.float32)
                + blend * updates[:, place]
            ).astype(jnp.bfloat16)
            if turn == 0:
                renewed[side] = rows
            pair.append(rows)
        keys, values = pair
        first = pl.multiple_of(group * width, width)
        queries = stacked(
            [message[:, pl.ds(pl.multiple_of(2 * width + first, width), width)] for message in messages]
        )
        for head, result in enumerate(answer(queries, keys, values, head_dim)):
            place = pl.ds(
                pl.multiple_of(2 * width + first + head * head_dim, head_dim), head_dim
            )
            for slot in range(chips):
                answers[slot][:, place] = result[
                    slot * token_count : (slot + 1) * token_count
                ].astype(jnp.bfloat16)
    for slot in range(chips):
        answers[slot][:, : 2 * width] = kept_out[slot]


def attend_refreshed(
    step_index, messages, relayed, order, kept_out, stale, other_stale, head_dim
):
    chips = len(messages)
    token_count, columns = messages[0].shape
    whole = pl.BlockSpec(memory_space=pltpu.VMEM)
    *answers, renewed = pl.pallas_call(
        partial(refreshed_kernel, order, head_dim),
        in_specs=[pl.BlockSpec(memory_space=pltpu.SMEM)] + [whole] * (2 * chips + 3),
        out_specs=[whole] * (chips + 1),
        out_shape=[jax.ShapeDtypeStruct((token_count, columns // 2), jnp.bfloat16)] * chips
        + [jax.ShapeDtypeStruct(stale.shape[1:], jnp.bfloat16)],
        scratch_shapes=[pltpu.VMEM((stale.shape[2], columns // 2), jnp.float32)],
        compiler_params=pltpu.CompilerParams(vmem_limit_bytes=VMEM_BYTES),
    )(step_index, *messages, *relayed, kept_out, stale, other_stale)
    return answers, renewed


def store_kernel(step_ref, stale_ref, renewed_ref, out_ref, sems):
    kept, refreshed = layers_of(step_ref[0])
    wait_all(
        start_all(
            [
                pltpu.make_async_copy(stale_ref.at[kept], out_ref.at[kept], sems.at[0]),
                pltpu.make_async_copy(renewed_ref, out_ref.at[refreshed], sems.at[1]),
            ]
        )
    )


def store(step_index, stale, renewed):
    far = pl.BlockSpec(memory_space=pl.ANY)
    return pl.pallas_call(
        store_kernel,
        in_specs=[pl.BlockSpec(memory_space=pltpu.SMEM)]
        + [pl.BlockSpec(memory_space=pltpu.VMEM)] * 2,
        out_specs=far,
        out_shape=jax.ShapeDtypeStruct(stale.shape, stale.dtype),
        scratch_shapes=[pltpu.SemaphoreType.DMA((2,))],
        compiler_params=pltpu.CompilerParams(vmem_limit_bytes=VMEM_BYTES),
    )(step_index, stale, renewed)


def after(array, *others):
    return lax.optimization_barrier((array, *others))[0]


def place_kernel(order, step_ref, *refs):
    chips = len(order)
    answers = refs[:chips]
    out_ref, placed, sems = refs[chips:]
    width = answers[0].shape[-1] // 2
    here = lax.div(lax.axis_index("patch"), 2)
    copies = []
    for half, layer in enumerate(layers_of(step_ref[0])):
        for slot, chip in enumerate(order):
            first = pl.multiple_of(lax.bitwise_xor(here, chip) * width, width)
            placed[layer, :, pl.ds(first, width)] = answers[slot][
                :, half * width : (half + 1) * width
            ]
        copies.append(
            pltpu.make_async_copy(placed.at[layer], out_ref.at[layer], sems.at[half])
        )
        copies[-1].start()
    wait_all(copies)


def place(step_index, answers, order):
    token_count, columns = answers[0].shape
    attended = jax.ShapeDtypeStruct((2, token_count, len(order) * columns // 2), jnp.bfloat16)
    return pl.pallas_call(
        partial(place_kernel, order),
        in_specs=[pl.BlockSpec(memory_space=pltpu.SMEM)]
        + [pl.BlockSpec(memory_space=pltpu.VMEM)] * len(order),
        out_specs=pl.BlockSpec(memory_space=pl.ANY),
        out_shape=attended,
        scratch_shapes=[
            pltpu.VMEM(attended.shape, attended.dtype),
            pltpu.SemaphoreType.DMA((2,)),
        ],
        compiler_params=pltpu.CompilerParams(vmem_limit_bytes=VMEM_BYTES),
    )(step_index, *answers)


def distances(chips):
    if chips == 8:
        return [5, 1, 3, 4, 6, 2, 7, 0], [7, 6, 5, 4, 3, 2, 1, 0]
    order = list(range(chips - 1, -1, -1))
    return order, order


def whole_key_body(
    queries, current_pairs, earlier_pairs, stale_cache, block_exponents, step_index
):
    devices = lax.axis_size("patch")
    chips = devices // 2
    layer_count, token_count, channel_count = queries.shape
    head_dim = channel_count // block_exponents.shape[-1]
    stale = stale_cache.reshape(layer_count, 2, devices * token_count, -1)
    order, back_order = distances(chips)
    other_stale = pairwise(stale, 1, devices)
    messages = pack(
        step_index, queries, current_pairs, earlier_pairs, block_exponents, order
    )
    *messages, other_stale = lax.optimization_barrier((*messages, other_stale))
    arrived = {
        chip: pairwise(messages[chip], 2 * chip, devices) for chip in order if chip
    }
    arrived[0] = messages[0]
    kept_out = attend_kept(
        step_index, queries, arrived, order, stale, other_stale, head_dim
    )
    arrived = [arrived[chip] for chip in order]
    relayed = [pairwise(message, 1, devices) for message in arrived]
    answers, renewed = attend_refreshed(
        step_index, arrived, relayed, order, kept_out, stale, other_stale, head_dim
    )
    by_chip = [answers[order.index(chip)] for chip in range(chips)]
    returned = [
        pairwise(by_chip[chip], 2 * chip, devices) if chip else by_chip[0] for chip in back_order
    ]
    renewed = store(step_index, stale, after(renewed, returned[0]))
    attended = place(step_index, returned, back_order)
    return attended, renewed.reshape(stale_cache.shape)


def exchange(rows):
    return lax.all_to_all(rows, "patch", split_axis=0, concat_axis=0, tiled=True)


def answer_part(blocks, key_rows, value_rows):
    score_scale = key_rows.shape[-1] ** (-0.5)

    def one_block(query_block):
        scores = (
            jnp.einsum("qhd,khd->hqk", query_block, key_rows, preferred_element_type=jnp.float32)
            * score_scale
        )
        peak = jnp.max(scores, -1, keepdims=True)
        weights = jnp.exp(scores - peak)
        total = jnp.sum(weights, -1)
        mixed = jnp.einsum(
            "hqk,khd->qhd",
            weights.astype(jnp.bfloat16),
            value_rows,
            preferred_element_type=jnp.float32,
        )
        return mixed / total.T[..., None], (peak[..., 0] + jnp.log(total)).T

    return lax.map(one_block, blocks)


def split_key_body(
    queries, current_pairs, earlier_pairs, stale_cache, block_exponents, step_index
):
    devices = lax.axis_size("patch")
    layer_count, token_count, channel_count = queries.shape
    head_count = block_exponents.shape[-1]
    head_dim = channel_count // head_count
    group_count = min(head_count, devices)
    part_count = devices // group_count
    group_heads = head_count // group_count
    part_rows = token_count // part_count
    width = group_heads * head_dim
    selector = step_index[0] % 2
    blend = blend_of(step_index[0])
    limits = block_limits(block_exponents)[..., None]
    residual = (current_pairs.astype(jnp.float32) - earlier_pairs.astype(jnp.float32)).reshape(
        layer_count, 2, token_count, head_count, head_dim
    )
    update = jnp.clip(residual, -limits, limits).astype(jnp.bfloat16)
    pieces = update.reshape(layer_count, 2, part_count, part_rows, group_count, width)
    pieces = pieces.transpose(0, 4, 2, 1, 3, 5).reshape(
        layer_count, devices, 2 * part_rows, width
    )
    asked = queries.reshape(layer_count, token_count, group_count, 1, width)
    asked = jnp.broadcast_to(
        asked.transpose(0, 2, 3, 1, 4),
        (layer_count, group_count, part_count, token_count, width),
    ).reshape(layer_count, devices, token_count, width)
    attended_list = []
    renewed_list = []
    for layer in range(layer_count):
        refresh = selector != layer % 2
        outgoing = jnp.where(refresh, pieces[layer], jnp.zeros_like(pieces[layer]))
        arrived = exchange(jnp.concatenate([outgoing, asked[layer]], 1))
        arrived_update = arrived[:, : 2 * part_rows].reshape(devices, 2, part_rows, width)
        renewed = (
            stale_cache[layer, :, 0].astype(jnp.float32)
            + blend * arrived_update.transpose(1, 0, 2, 3).astype(jnp.float32)
        ).astype(jnp.bfloat16)
        key_rows = renewed[0].reshape(devices * part_rows, group_heads, head_dim)
        value_rows = renewed[1].reshape(devices * part_rows, group_heads, head_dim)
        block_span = 1
        while (
            block_span * token_count < 512 and devices % (2 * block_span) == 0
        ):
            block_span = block_span * 2
        blocks = arrived[:, 2 * part_rows :].reshape(
            devices // block_span, block_span * token_count, group_heads, head_dim
        )
        partial_out, log_total = answer_part(blocks, key_rows, value_rows)
        back_out = exchange(
            partial_out.astype(jnp.bfloat16).reshape(devices, token_count, width)
        ).astype(jnp.float32)
        back_log = exchange(
            log_total.astype(jnp.bfloat16).reshape(devices, token_count, group_heads)
        ).astype(jnp.float32)
        back_out = back_out.reshape(group_count, part_count, token_count, group_heads, head_dim)
        back_log = back_log.reshape(group_count, part_count, token_count, group_heads)
        factor = jnp.exp(back_log - jnp.max(back_log, 1, keepdims=True))
        merged = jnp.sum(factor[..., None] * back_out, 1) / jnp.sum(factor, 1)[..., None]
        attended_list.append(
            merged.transpose(1, 0, 2, 3)
            .reshape(token_count, channel_count)
            .astype(jnp.bfloat16)
        )
        renewed_list.append(renewed)
    return jnp.stack(attended_list), jnp.stack(renewed_list)[:, :, None]


def body(queries, current_pairs, earlier_pairs, stale_cache, block_exponents, step_index):
    layer_count = queries.shape[0]
    head_count = block_exponents.shape[-1]
    devices = lax.axis_size("patch")
    one_part = 1 < devices <= head_count and devices & (devices - 1) == 0 and layer_count == 2
    chosen = whole_key_body if one_part else split_key_body
    return chosen(
        queries, current_pairs, earlier_pairs, stale_cache, block_exponents, step_index
    )


def solution(mesh):
    in_specs = (
        P(None, ("groups", "patch"), None),
        P(None, None, ("groups", "patch"), None),
        P(None, None, ("groups", "patch"), None),
        P(None, None, ("groups", "patch"), None, None, None),
        P(None, None, ("groups", "patch"), None),
        P("groups"),
    )
    out_specs = (
        P(None, ("groups", "patch"), None),
        P(None, None, ("groups", "patch"), None, None, None),
    )
    return jax.shard_map(body, mesh=mesh, in_specs=in_specs, out_specs=out_specs, check_vma=False)
```

```python
from functools import partial

import jax
import jax.numpy as jnp
from jax import lax
from jax.experimental import pallas as pl
from jax.experimental.pallas import tpu as pltpu
from jax.sharding import PartitionSpec as P

STEPS = 50
SATURATION = 448
TOP_LEVEL = 8
VMEM_BYTES = 40 * 1024 * 1024
PACK_BYTES = 60 * 1024 * 1024


def block_limits(exponents):
    return ((SATURATION << TOP_LEVEL) >> exponents).astype(jnp.float32) * (2.0**-TOP_LEVEL)


def blend_of(step):
    return 1.0 - step.astype(jnp.float32) / (2.0 * STEPS)


def layers_of(step):
    kept = lax.rem(step, 2)
    return kept, 1 - kept


def pairwise(array, distance, devices):
    pairs = [(device, device ^ distance) for device in range(devices)]
    return lax.ppermute(array, "patch", pairs)


def start_all(copies):
    for copy in copies:
        copy.start()
    return copies


def wait_all(copies):
    for copy in copies:
        copy.wait()


def pack_kernel(order, step_ref, query_ref, current_ref, earlier_ref, exponent_ref, *refs):
    chips = len(order)
    messages = refs[:chips]
    queries, current, earlier, exponents, limits, sems, side_sems = refs[chips:]
    _, _, channel_count = query_ref.shape
    head_count = exponent_ref.shape[-1]
    head_dim = channel_count // head_count
    width = channel_count // chips
    kept, refreshed = layers_of(step_ref[0])
    here = lax.div(lax.axis_index("patch"), 2)
    copies = start_all(
        [
            pltpu.make_async_copy(exponent_ref.at[refreshed], exponents, sems.at[0]),
            pltpu.make_async_copy(query_ref, queries, sems.at[1]),
        ]
    )
    pair_copies = start_all(
        [
            pltpu.make_async_copy(source.at[refreshed], target, side_sems.at[index])
            for index, (source, target) in enumerate(
                ((current_ref, current), (earlier_ref, earlier))
            )
        ]
    )
    copies[0].wait()
    for side in range(2):
        values = block_limits(exponents[side])
        for head in range(head_count):
            limits[side, :, head * head_dim : (head + 1) * head_dim] = jnp.broadcast_to(
                values[:, head : head + 1], (values.shape[0], head_dim)
            )
    copies[1].wait()
    spans = [
        pl.ds(pl.multiple_of(lax.bitwise_xor(here, chip) * width, width), width)
        for chip in order
    ]
    for chip, span in zip(order, spans):
        for slot, layer in enumerate((kept, refreshed)):
            messages[chip][:, slot * width : (slot + 1) * width] = queries[layer, :, span]
    for side in range(2):
        if side == 0:
            wait_all(pair_copies)
        for chip, span in zip(order, spans):
            residual = current[side, :, span].astype(jnp.float32) - earlier[
                side, :, span
            ].astype(jnp.float32)
            limit = limits[side, :, span]
            update = jnp.minimum(jnp.maximum(residual, -limit), limit).astype(jnp.bfloat16)
            messages[chip][:, (2 + side) * width : (3 + side) * width] = update


def pack(step_index, queries, current_pairs, earlier_pairs, block_exponents, order):
    _, token_count, channel_count = queries.shape
    chips = len(order)
    columns = 4 * (channel_count // chips)
    far = pl.BlockSpec(memory_space=pl.ANY)
    layers = [current_pairs, earlier_pairs, block_exponents]
    return pl.pallas_call(
        partial(pack_kernel, order),
        in_specs=[pl.BlockSpec(memory_space=pltpu.SMEM)] + [far] * 4,
        out_specs=[pl.BlockSpec(memory_space=pltpu.VMEM)] * chips,
        out_shape=[jax.ShapeDtypeStruct((token_count, columns), jnp.bfloat16)] * chips,
        scratch_shapes=[pltpu.VMEM(queries.shape, queries.dtype)]
        + [pltpu.VMEM(array.shape[1:], array.dtype) for array in layers]
        + [
            pltpu.VMEM(current_pairs.shape[1:], jnp.float32),
            pltpu.SemaphoreType.DMA((2,)),
            pltpu.SemaphoreType.DMA((2,)),
        ],
        compiler_params=pltpu.CompilerParams(vmem_limit_bytes=PACK_BYTES),
    )(step_index, queries, current_pairs, earlier_pairs, block_exponents)


def stacked(blocks):
    return jnp.concatenate([block.astype(jnp.float32) for block in blocks], 0).astype(
        jnp.bfloat16
    )


def answer(queries, keys, values, head_dim):
    spans = [
        slice(first, first + head_dim) for first in range(0, queries.shape[-1], head_dim)
    ]
    scores = [
        lax.dot_general(
            queries[:, span],
            keys[:, span],
            (((1,), (1,)), ((), ())),
            preferred_element_type=jnp.float32,
        )
        for span in spans
    ]
    weights = [
        jnp.exp((score - jnp.max(score, -1, keepdims=True)) * head_dim ** (-0.5))
        for score in scores
    ]
    return [
        jnp.dot(weight.astype(jnp.bfloat16), values[:, span], preferred_element_type=jnp.float32)
        / jnp.sum(weight, -1, keepdims=True)
        for weight, span in zip(weights, spans)
    ]


def kept_kernel(order, head_dim, step_ref, query_ref, *refs):
    messages = dict(zip([chip for chip in order if chip], refs))
    own_ref, other_ref, out_ref = refs[len(messages) :]
    token_count = query_ref.shape[1]
    width = own_ref.shape[-1]
    kept, _ = layers_of(step_ref[0])
    here, core = lax.div(lax.axis_index("patch"), 2), lax.rem(lax.axis_index("patch"), 2)
    for group, cache_ref in ((core, own_ref), (1 - core, other_ref)):
        first = pl.multiple_of(group * width, width)
        blocks = []
        for chip in order:
            if chip:
                blocks.append(messages[chip][:, pl.ds(first, width)])
            else:
                place = pl.multiple_of((2 * here + group) * width, width)
                blocks.append(query_ref[kept, :, pl.ds(place, width)])
        queries = stacked(blocks)
        keys, values = cache_ref[kept, 0], cache_ref[kept, 1]
        for head, result in enumerate(answer(queries, keys, values, head_dim)):
            place = pl.ds(pl.multiple_of(first + head * head_dim, head_dim), head_dim)
            for slot in range(len(order)):
                out_ref[slot, :, place] = result[
                    slot * token_count : (slot + 1) * token_count
                ].astype(jnp.bfloat16)


def attend_kept(step_index, queries, arrived, order, stale, other_stale, head_dim):
    chips = len(order)
    messages = [arrived[chip] for chip in order if chip]
    _, token_count, channel_count = queries.shape
    whole = pl.BlockSpec(memory_space=pltpu.VMEM)
    return pl.pallas_call(
        partial(kept_kernel, order, head_dim),
        in_specs=[pl.BlockSpec(memory_space=pltpu.SMEM)] + [whole] * (chips + 2),
        out_specs=whole,
        out_shape=jax.ShapeDtypeStruct(
            (chips, token_count, channel_count // chips), jnp.bfloat16
        ),
        compiler_params=pltpu.CompilerParams(vmem_limit_bytes=VMEM_BYTES),
    )(step_index, queries, *messages, stale, other_stale)


def refreshed_kernel(order, head_dim, step_ref, *refs):
    chips = len(order)
    messages, relayed = refs[:chips], refs[chips : 2 * chips]
    kept_out, own_ref, other_ref = refs[2 * chips : 2 * chips + 3]
    answers = refs[2 * chips + 3 : 3 * chips + 3]
    renewed, updates = refs[3 * chips + 3 :]
    width = own_ref.shape[-1]
    token_count = messages[0].shape[0]
    step = step_ref[0]
    _, refreshed = layers_of(step)
    blend = blend_of(step)
    me = lax.axis_index("patch")
    core = lax.rem(me, 2)
    for slot, chip in enumerate(order):
        for source, message in ((2 * chip, messages[slot]), (2 * chip + 1, relayed[slot])):
            row = pl.multiple_of(lax.bitwise_xor(me, source) * token_count, 8)
            updates[pl.ds(row, token_count), :] = message[:, 4 * width :].astype(jnp.float32)
    results = []
    for turn, (group, cache_ref) in enumerate(((core, own_ref), (1 - core, other_ref))):
        pair = []
        for side in range(2):
            place = pl.ds(pl.multiple_of((2 * side + group) * width, width), width)
            rows = (
                cache_ref[refreshed, side].astype(jnp.float32)
                + blend * updates[:, place]
            ).astype(jnp.bfloat16)
            if turn == 0:
                renewed[side] = rows
            pair.append(rows)
        keys, values = pair
        first = pl.multiple_of(group * width, width)
        queries = stacked(
            [message[:, pl.ds(pl.multiple_of(2 * width + first, width), width)] for message in messages]
        )
        for head, result in enumerate(answer(queries, keys, values, head_dim)):
            place = pl.ds(
                pl.multiple_of(2 * width + first + head * head_dim, head_dim), head_dim
            )
            for slot in range(chips):
                answers[slot][:, place] = result[
                    slot * token_count : (slot + 1) * token_count
                ].astype(jnp.bfloat16)
    for slot in range(chips):
        answers[slot][:, : 2 * width] = kept_out[slot]


def attend_refreshed(
    step_index, messages, relayed, order, kept_out, stale, other_stale, head_dim
):
    chips = len(messages)
    token_count, columns = messages[0].shape
    whole = pl.BlockSpec(memory_space=pltpu.VMEM)
    *answers, renewed = pl.pallas_call(
        partial(refreshed_kernel, order, head_dim),
        in_specs=[pl.BlockSpec(memory_space=pltpu.SMEM)] + [whole] * (2 * chips + 3),
        out_specs=[whole] * (chips + 1),
        out_shape=[jax.ShapeDtypeStruct((token_count, columns // 2), jnp.bfloat16)] * chips
        + [jax.ShapeDtypeStruct(stale.shape[1:], jnp.bfloat16)],
        scratch_shapes=[pltpu.VMEM((stale.shape[2], columns // 2), jnp.float32)],
        compiler_params=pltpu.CompilerParams(vmem_limit_bytes=VMEM_BYTES),
    )(step_index, *messages, *relayed, kept_out, stale, other_stale)
    return answers, renewed


def store_kernel(step_ref, stale_ref, renewed_ref, out_ref, sems):
    kept, refreshed = layers_of(step_ref[0])
    wait_all(
        start_all(
            [
                pltpu.make_async_copy(stale_ref.at[kept], out_ref.at[kept], sems.at[0]),
                pltpu.make_async_copy(renewed_ref, out_ref.at[refreshed], sems.at[1]),
            ]
        )
    )


def store(step_index, stale, renewed):
    far = pl.BlockSpec(memory_space=pl.ANY)
    return pl.pallas_call(
        store_kernel,
        in_specs=[pl.BlockSpec(memory_space=pltpu.SMEM)]
        + [pl.BlockSpec(memory_space=pltpu.VMEM)] * 2,
        out_specs=far,
        out_shape=jax.ShapeDtypeStruct(stale.shape, stale.dtype),
        scratch_shapes=[pltpu.SemaphoreType.DMA((2,))],
        compiler_params=pltpu.CompilerParams(vmem_limit_bytes=VMEM_BYTES),
    )(step_index, stale, renewed)


def after(array, *others):
    return lax.optimization_barrier((array, *others))[0]


def place_kernel(order, step_ref, *refs):
    chips = len(order)
    answers = refs[:chips]
    out_ref, placed, sems = refs[chips:]
    width = answers[0].shape[-1] // 2
    here = lax.div(lax.axis_index("patch"), 2)
    copies = []
    for half, layer in enumerate(layers_of(step_ref[0])):
        for slot, chip in enumerate(order):
            first = pl.multiple_of(lax.bitwise_xor(here, chip) * width, width)
            placed[layer, :, pl.ds(first, width)] = answers[slot][
                :, half * width : (half + 1) * width
            ]
        copies.append(
            pltpu.make_async_copy(placed.at[layer], out_ref.at[layer], sems.at[half])
        )
        copies[-1].start()
    wait_all(copies)


def place(step_index, answers, order):
    token_count, columns = answers[0].shape
    attended = jax.ShapeDtypeStruct((2, token_count, len(order) * columns // 2), jnp.bfloat16)
    return pl.pallas_call(
        partial(place_kernel, order),
        in_specs=[pl.BlockSpec(memory_space=pltpu.SMEM)]
        + [pl.BlockSpec(memory_space=pltpu.VMEM)] * len(order),
        out_specs=pl.BlockSpec(memory_space=pl.ANY),
        out_shape=attended,
        scratch_shapes=[
            pltpu.VMEM(attended.shape, attended.dtype),
            pltpu.SemaphoreType.DMA((2,)),
        ],
        compiler_params=pltpu.CompilerParams(vmem_limit_bytes=VMEM_BYTES),
    )(step_index, *answers)


def distances(chips):
    if chips == 8:
        return [5, 1, 3, 4, 6, 2, 7, 0], [7, 6, 5, 4, 3, 2, 1, 0]
    order = list(range(chips - 1, -1, -1))
    return order, order


def whole_key_body(
    queries, current_pairs, earlier_pairs, stale_cache, block_exponents, step_index
):
    devices = lax.axis_size("patch")
    chips = devices // 2
    layer_count, token_count, channel_count = queries.shape
    head_dim = channel_count // block_exponents.shape[-1]
    stale = stale_cache.reshape(layer_count, 2, devices * token_count, -1)
    order, back_order = distances(chips)
    other_stale = pairwise(stale, 1, devices)
    messages = pack(
        step_index, queries, current_pairs, earlier_pairs, block_exponents, order
    )
    *messages, other_stale = lax.optimization_barrier((*messages, other_stale))
    arrived = {
        chip: pairwise(messages[chip], 2 * chip, devices) for chip in order if chip
    }
    arrived[0] = messages[0]
    kept_out = attend_kept(
        step_index, queries, arrived, order, stale, other_stale, head_dim
    )
    arrived = [arrived[chip] for chip in order]
    relayed = [pairwise(message, 1, devices) for message in arrived]
    answers, renewed = attend_refreshed(
        step_index, arrived, relayed, order, kept_out, stale, other_stale, head_dim
    )
    by_chip = [answers[order.index(chip)] for chip in range(chips)]
    returned = [
        pairwise(by_chip[chip], 2 * chip, devices) if chip else by_chip[0] for chip in back_order
    ]
    renewed = store(step_index, stale, after(renewed, returned[0]))
    attended = place(step_index, returned, back_order)
    return attended, renewed.reshape(stale_cache.shape)


def exchange(rows):
    return lax.all_to_all(rows, "patch", split_axis=0, concat_axis=0, tiled=True)


def answer_part(blocks, key_rows, value_rows):
    score_scale = key_rows.shape[-1] ** (-0.5)

    def one_block(query_block):
        scores = (
            jnp.einsum("qhd,khd->hqk", query_block, key_rows, preferred_element_type=jnp.float32)
            * score_scale
        )
        peak = jnp.max(scores, -1, keepdims=True)
        weights = jnp.exp(scores - peak)
        total = jnp.sum(weights, -1)
        mixed = jnp.einsum(
            "hqk,khd->qhd",
            weights.astype(jnp.bfloat16),
            value_rows,
            preferred_element_type=jnp.float32,
        )
        return mixed / total.T[..., None], (peak[..., 0] + jnp.log(total)).T

    return lax.map(one_block, blocks)


def split_key_body(
    queries, current_pairs, earlier_pairs, stale_cache, block_exponents, step_index
):
    devices = lax.axis_size("patch")
    layer_count, token_count, channel_count = queries.shape
    head_count = block_exponents.shape[-1]
    head_dim = channel_count // head_count
    group_count = min(head_count, devices)
    part_count = devices // group_count
    group_heads = head_count // group_count
    part_rows = token_count // part_count
    width = group_heads * head_dim
    selector = step_index[0] % 2
    blend = blend_of(step_index[0])
    limits = block_limits(block_exponents)[..., None]
    residual = (current_pairs.astype(jnp.float32) - earlier_pairs.astype(jnp.float32)).reshape(
        layer_count, 2, token_count, head_count, head_dim
    )
    update = jnp.clip(residual, -limits, limits).astype(jnp.bfloat16)
    pieces = update.reshape(layer_count, 2, part_count, part_rows, group_count, width)
    pieces = pieces.transpose(0, 4, 2, 1, 3, 5).reshape(
        layer_count, devices, 2 * part_rows, width
    )
    asked = queries.reshape(layer_count, token_count, group_count, 1, width)
    asked = jnp.broadcast_to(
        asked.transpose(0, 2, 3, 1, 4),
        (layer_count, group_count, part_count, token_count, width),
    ).reshape(layer_count, devices, token_count, width)
    attended_list = []
    renewed_list = []
    for layer in range(layer_count):
        refresh = selector != layer % 2
        outgoing = jnp.where(refresh, pieces[layer], jnp.zeros_like(pieces[layer]))
        arrived = exchange(jnp.concatenate([outgoing, asked[layer]], 1))
        arrived_update = arrived[:, : 2 * part_rows].reshape(devices, 2, part_rows, width)
        renewed = (
            stale_cache[layer, :, 0].astype(jnp.float32)
            + blend * arrived_update.transpose(1, 0, 2, 3).astype(jnp.float32)
        ).astype(jnp.bfloat16)
        key_rows = renewed[0].reshape(devices * part_rows, group_heads, head_dim)
        value_rows = renewed[1].reshape(devices * part_rows, group_heads, head_dim)
        block_span = 1
        while (
            block_span * token_count < 512 and devices % (2 * block_span) == 0
        ):
            block_span = block_span * 2
        blocks = arrived[:, 2 * part_rows :].reshape(
            devices // block_span, block_span * token_count, group_heads, head_dim
        )
        partial_out, log_total = answer_part(blocks, key_rows, value_rows)
        back_out = exchange(
            partial_out.astype(jnp.bfloat16).reshape(devices, token_count, width)
        ).astype(jnp.float32)
        back_log = exchange(
            log_total.astype(jnp.bfloat16).reshape(devices, token_count, group_heads)
        ).astype(jnp.float32)
        back_out = back_out.reshape(group_count, part_count, token_count, group_heads, head_dim)
        back_log = back_log.reshape(group_count, part_count, token_count, group_heads)
        factor = jnp.exp(back_log - jnp.max(back_log, 1, keepdims=True))
        merged = jnp.sum(factor[..., None] * back_out, 1) / jnp.sum(factor, 1)[..., None]
        attended_list.append(
            merged.transpose(1, 0, 2, 3)
            .reshape(token_count, channel_count)
            .astype(jnp.bfloat16)
        )
        renewed_list.append(renewed)
    return jnp.stack(attended_list), jnp.stack(renewed_list)[:, :, None]


def body(queries, current_pairs, earlier_pairs, stale_cache, block_exponents, step_index):
    layer_count = queries.shape[0]
    head_count = block_exponents.shape[-1]
    devices = lax.axis_size("patch")
    one_part = 1 < devices <= head_count and devices & (devices - 1) == 0 and layer_count == 2
    chosen = whole_key_body if one_part else split_key_body
    return chosen(
        queries, current_pairs, earlier_pairs, stale_cache, block_exponents, step_index
    )


def solution(mesh):
    in_specs = (
        P(None, ("groups", "patch"), None),
        P(None, None, ("groups", "patch"), None),
        P(None, None, ("groups", "patch"), None),
        P(None, None, ("groups", "patch"), None, None, None),
        P(None, None, ("groups", "patch"), None),
        P("groups"),
    )
    out_specs = (
        P(None, ("groups", "patch"), None),
        P(None, None, ("groups", "patch"), None, None, None),
    )
    return jax.shard_map(body, mesh=mesh, in_specs=in_specs, out_specs=out_specs, check_vma=False)
```

```python
from functools import partial

import jax
import jax.numpy as jnp
from jax import lax
from jax.experimental import pallas as pl
from jax.experimental.pallas import tpu as pltpu
from jax.sharding import PartitionSpec as P

STEPS = 50
SATURATION = 448
TOP_LEVEL = 8
VMEM_BYTES = 40 * 1024 * 1024
PACK_BYTES = 60 * 1024 * 1024


def block_limits(exponents):
    return ((SATURATION << TOP_LEVEL) >> exponents).astype(jnp.float32) * (2.0**-TOP_LEVEL)


def blend_of(step):
    return 1.0 - step.astype(jnp.float32) / (2.0 * STEPS)


def layers_of(step):
    kept = lax.rem(step, 2)
    return kept, 1 - kept


def pairwise(array, distance, devices):
    pairs = [(device, device ^ distance) for device in range(devices)]
    return lax.ppermute(array, "patch", pairs)


def start_all(copies):
    for copy in copies:
        copy.start()
    return copies


def wait_all(copies):
    for copy in copies:
        copy.wait()


def pack_kernel(order, step_ref, query_ref, current_ref, earlier_ref, exponent_ref, *refs):
    chips = len(order)
    messages = refs[:chips]
    queries, current, earlier, exponents, limits, sems, side_sems = refs[chips:]
    _, _, channel_count = query_ref.shape
    head_count = exponent_ref.shape[-1]
    head_dim = channel_count // head_count
    width = channel_count // chips
    kept, refreshed = layers_of(step_ref[0])
    here = lax.div(lax.axis_index("patch"), 2)
    copies = start_all(
        [
            pltpu.make_async_copy(exponent_ref.at[refreshed], exponents, sems.at[0]),
            pltpu.make_async_copy(query_ref, queries, sems.at[1]),
        ]
    )
    pair_copies = start_all(
        [
            pltpu.make_async_copy(source.at[refreshed], target, side_sems.at[index])
            for index, (source, target) in enumerate(
                ((current_ref, current), (earlier_ref, earlier))
            )
        ]
    )
    copies[0].wait()
    for side in range(2):
        values = block_limits(exponents[side])
        for head in range(head_count):
            limits[side, :, head * head_dim : (head + 1) * head_dim] = jnp.broadcast_to(
                values[:, head : head + 1], (values.shape[0], head_dim)
            )
    copies[1].wait()
    spans = [
        pl.ds(pl.multiple_of(lax.bitwise_xor(here, chip) * width, width), width)
        for chip in order
    ]
    for chip, span in zip(order, spans):
        for slot, layer in enumerate((kept, refreshed)):
            messages[chip][:, slot * width : (slot + 1) * width] = queries[layer, :, span]
    for side in range(2):
        if side == 0:
            wait_all(pair_copies)
        for chip, span in zip(order, spans):
            residual = current[side, :, span].astype(jnp.float32) - earlier[
                side, :, span
            ].astype(jnp.float32)
            limit = limits[side, :, span]
            update = jnp.minimum(jnp.maximum(residual, -limit), limit).astype(jnp.bfloat16)
            messages[chip][:, (2 + side) * width : (3 + side) * width] = update


def pack(step_index, queries, current_pairs, earlier_pairs, block_exponents, order):
    _, token_count, channel_count = queries.shape
    chips = len(order)
    columns = 4 * (channel_count // chips)
    far = pl.BlockSpec(memory_space=pl.ANY)
    layers = [current_pairs, earlier_pairs, block_exponents]
    return pl.pallas_call(
        partial(pack_kernel, order),
        in_specs=[pl.BlockSpec(memory_space=pltpu.SMEM)] + [far] * 4,
        out_specs=[pl.BlockSpec(memory_space=pltpu.VMEM)] * chips,
        out_shape=[jax.ShapeDtypeStruct((token_count, columns), jnp.bfloat16)] * chips,
        scratch_shapes=[pltpu.VMEM(queries.shape, queries.dtype)]
        + [pltpu.VMEM(array.shape[1:], array.dtype) for array in layers]
        + [
            pltpu.VMEM(current_pairs.shape[1:], jnp.float32),
            pltpu.SemaphoreType.DMA((2,)),
            pltpu.SemaphoreType.DMA((2,)),
        ],
        compiler_params=pltpu.CompilerParams(vmem_limit_bytes=PACK_BYTES),
    )(step_index, queries, current_pairs, earlier_pairs, block_exponents)


def stacked(blocks):
    return jnp.concatenate([block.astype(jnp.float32) for block in blocks], 0).astype(
        jnp.bfloat16
    )


def answer(queries, keys, values, head_dim):
    spans = [
        slice(first, first + head_dim) for first in range(0, queries.shape[-1], head_dim)
    ]
    scores = [
        lax.dot_general(
            queries[:, span],
            keys[:, span],
            (((1,), (1,)), ((), ())),
            preferred_element_type=jnp.float32,
        )
        for span in spans
    ]
    weights = [
        jnp.exp((score - jnp.max(score, -1, keepdims=True)) * head_dim ** (-0.5))
        for score in scores
    ]
    return [
        jnp.dot(weight.astype(jnp.bfloat16), values[:, span], preferred_element_type=jnp.float32)
        / jnp.sum(weight, -1, keepdims=True)
        for weight, span in zip(weights, spans)
    ]


def kept_kernel(order, head_dim, step_ref, query_ref, *refs):
    messages = dict(zip([chip for chip in order if chip], refs))
    own_ref, other_ref, out_ref = refs[len(messages) :]
    token_count = query_ref.shape[1]
    width = own_ref.shape[-1]
    kept, _ = layers_of(step_ref[0])
    here, core = lax.div(lax.axis_index("patch"), 2), lax.rem(lax.axis_index("patch"), 2)
    for group, cache_ref in ((core, own_ref), (1 - core, other_ref)):
        first = pl.multiple_of(group * width, width)
        blocks = []
        for chip in order:
            if chip:
                blocks.append(messages[chip][:, pl.ds(first, width)])
            else:
                place = pl.multiple_of((2 * here + group) * width, width)
                blocks.append(query_ref[kept, :, pl.ds(place, width)])
        queries = stacked(blocks)
        keys, values = cache_ref[kept, 0], cache_ref[kept, 1]
        for head, result in enumerate(answer(queries, keys, values, head_dim)):
            place = pl.ds(pl.multiple_of(first + head * head_dim, head_dim), head_dim)
            for slot in range(len(order)):
                out_ref[slot, :, place] = result[
                    slot * token_count : (slot + 1) * token_count
                ].astype(jnp.bfloat16)


def attend_kept(step_index, queries, arrived, order, stale, other_stale, head_dim):
    chips = len(order)
    messages = [arrived[chip] for chip in order if chip]
    _, token_count, channel_count = queries.shape
    whole = pl.BlockSpec(memory_space=pltpu.VMEM)
    return pl.pallas_call(
        partial(kept_kernel, order, head_dim),
        in_specs=[pl.BlockSpec(memory_space=pltpu.SMEM)] + [whole] * (chips + 2),
        out_specs=whole,
        out_shape=jax.ShapeDtypeStruct(
            (chips, token_count, channel_count // chips), jnp.bfloat16
        ),
        compiler_params=pltpu.CompilerParams(vmem_limit_bytes=VMEM_BYTES),
    )(step_index, queries, *messages, stale, other_stale)


def refreshed_kernel(order, head_dim, step_ref, *refs):
    chips = len(order)
    messages, relayed = refs[:chips], refs[chips : 2 * chips]
    kept_out, own_ref, other_ref = refs[2 * chips : 2 * chips + 3]
    answers = refs[2 * chips + 3 : 3 * chips + 3]
    renewed, updates = refs[3 * chips + 3 :]
    width = own_ref.shape[-1]
    token_count = messages[0].shape[0]
    step = step_ref[0]
    _, refreshed = layers_of(step)
    blend = blend_of(step)
    me = lax.axis_index("patch")
    core = lax.rem(me, 2)
    for slot, chip in enumerate(order):
        for source, message in ((2 * chip, messages[slot]), (2 * chip + 1, relayed[slot])):
            row = pl.multiple_of(lax.bitwise_xor(me, source) * token_count, 8)
            updates[pl.ds(row, token_count), :] = message[:, 4 * width :].astype(jnp.float32)
    results = []
    for turn, (group, cache_ref) in enumerate(((core, own_ref), (1 - core, other_ref))):
        pair = []
        for side in range(2):
            place = pl.ds(pl.multiple_of((2 * side + group) * width, width), width)
            rows = (
                cache_ref[refreshed, side].astype(jnp.float32)
                + blend * updates[:, place]
            ).astype(jnp.bfloat16)
            if turn == 0:
                renewed[side] = rows
            pair.append(rows)
        keys, values = pair
        first = pl.multiple_of(group * width, width)
        queries = stacked(
            [message[:, pl.ds(pl.multiple_of(2 * width + first, width), width)] for message in messages]
        )
        for head, result in enumerate(answer(queries, keys, values, head_dim)):
            place = pl.ds(
                pl.multiple_of(2 * width + first + head * head_dim, head_dim), head_dim
            )
            for slot in range(chips):
                answers[slot][:, place] = result[
                    slot * token_count : (slot + 1) * token_count
                ].astype(jnp.bfloat16)
    for slot in range(chips):
        answers[slot][:, : 2 * width] = kept_out[slot]


def attend_refreshed(
    step_index, messages, relayed, order, kept_out, stale, other_stale, head_dim
):
    chips = len(messages)
    token_count, columns = messages[0].shape
    whole = pl.BlockSpec(memory_space=pltpu.VMEM)
    *answers, renewed = pl.pallas_call(
        partial(refreshed_kernel, order, head_dim),
        in_specs=[pl.BlockSpec(memory_space=pltpu.SMEM)] + [whole] * (2 * chips + 3),
        out_specs=[whole] * (chips + 1),
        out_shape=[jax.ShapeDtypeStruct((token_count, columns // 2), jnp.bfloat16)] * chips
        + [jax.ShapeDtypeStruct(stale.shape[1:], jnp.bfloat16)],
        scratch_shapes=[pltpu.VMEM((stale.shape[2], columns // 2), jnp.float32)],
        compiler_params=pltpu.CompilerParams(vmem_limit_bytes=VMEM_BYTES),
    )(step_index, *messages, *relayed, kept_out, stale, other_stale)
    return answers, renewed


def store_kernel(step_ref, stale_ref, renewed_ref, out_ref, sems):
    kept, refreshed = layers_of(step_ref[0])
    wait_all(
        start_all(
            [
                pltpu.make_async_copy(stale_ref.at[kept], out_ref.at[kept], sems.at[0]),
                pltpu.make_async_copy(renewed_ref, out_ref.at[refreshed], sems.at[1]),
            ]
        )
    )


def store(step_index, stale, renewed):
    far = pl.BlockSpec(memory_space=pl.ANY)
    return pl.pallas_call(
        store_kernel,
        in_specs=[pl.BlockSpec(memory_space=pltpu.SMEM)]
        + [pl.BlockSpec(memory_space=pltpu.VMEM)] * 2,
        out_specs=far,
        out_shape=jax.ShapeDtypeStruct(stale.shape, stale.dtype),
        scratch_shapes=[pltpu.SemaphoreType.DMA((2,))],
        compiler_params=pltpu.CompilerParams(vmem_limit_bytes=VMEM_BYTES),
    )(step_index, stale, renewed)


def after(array, *others):
    return lax.optimization_barrier((array, *others))[0]


def place_kernel(order, step_ref, *refs):
    *answers, out_ref = refs
    width = answers[0].shape[-1] // 2
    here = lax.div(lax.axis_index("patch"), 2)
    for half, layer in enumerate(layers_of(step_ref[0])):
        for slot, chip in enumerate(order):
            first = pl.multiple_of(lax.bitwise_xor(here, chip) * width, width)
            out_ref[layer, :, pl.ds(first, width)] = answers[slot][
                :, half * width : (half + 1) * width
            ]


def place(step_index, answers, order):
    token_count, columns = answers[0].shape
    attended = jax.ShapeDtypeStruct((2, token_count, len(order) * columns // 2), jnp.bfloat16)
    return pl.pallas_call(
        partial(place_kernel, order),
        in_specs=[pl.BlockSpec(memory_space=pltpu.SMEM)]
        + [pl.BlockSpec(memory_space=pltpu.VMEM)] * len(order),
        out_specs=pl.BlockSpec(memory_space=pltpu.VMEM),
        out_shape=attended,
        compiler_params=pltpu.CompilerParams(vmem_limit_bytes=VMEM_BYTES),
    )(step_index, *answers)


def distances(chips):
    if chips == 8:
        return [5, 3, 4, 6, 2, 1, 7, 0], [7, 6, 5, 4, 3, 2, 1, 0]
    order = list(range(chips - 1, -1, -1))
    return order, order


def whole_key_body(
    queries, current_pairs, earlier_pairs, stale_cache, block_exponents, step_index
):
    devices = lax.axis_size("patch")
    chips = devices // 2
    layer_count, token_count, channel_count = queries.shape
    head_dim = channel_count // block_exponents.shape[-1]
    stale = stale_cache.reshape(layer_count, 2, devices * token_count, -1)
    order, back_order = distances(chips)
    other_stale = pairwise(stale, 1, devices)
    messages = pack(
        step_index, queries, current_pairs, earlier_pairs, block_exponents, order
    )
    *messages, other_stale = lax.optimization_barrier((*messages, other_stale))
    arrived = {
        chip: pairwise(messages[chip], 2 * chip, devices) for chip in order if chip
    }
    arrived[0] = messages[0]
    kept_out = attend_kept(
        step_index, queries, arrived, order, stale, other_stale, head_dim
    )
    arrived = [arrived[chip] for chip in order]
    relayed = [pairwise(message, 1, devices) for message in arrived]
    answers, renewed = attend_refreshed(
        step_index, arrived, relayed, order, kept_out, stale, other_stale, head_dim
    )
    by_chip = [answers[order.index(chip)] for chip in range(chips)]
    returned = [
        pairwise(by_chip[chip], 2 * chip, devices) if chip else by_chip[0] for chip in back_order
    ]
    renewed = store(step_index, stale, after(renewed, returned[0]))
    attended = place(step_index, returned, back_order)
    return attended, renewed.reshape(stale_cache.shape)


def exchange(rows):
    return lax.all_to_all(rows, "patch", split_axis=0, concat_axis=0, tiled=True)


def answer_part(blocks, key_rows, value_rows):
    score_scale = key_rows.shape[-1] ** (-0.5)

    def one_block(query_block):
        scores = (
            jnp.einsum("qhd,khd->hqk", query_block, key_rows, preferred_element_type=jnp.float32)
            * score_scale
        )
        peak = jnp.max(scores, -1, keepdims=True)
        weights = jnp.exp(scores - peak)
        total = jnp.sum(weights, -1)
        mixed = jnp.einsum(
            "hqk,khd->qhd",
            weights.astype(jnp.bfloat16),
            value_rows,
            preferred_element_type=jnp.float32,
        )
        return mixed / total.T[..., None], (peak[..., 0] + jnp.log(total)).T

    return lax.map(one_block, blocks)


def split_key_body(
    queries, current_pairs, earlier_pairs, stale_cache, block_exponents, step_index
):
    devices = lax.axis_size("patch")
    layer_count, token_count, channel_count = queries.shape
    head_count = block_exponents.shape[-1]
    head_dim = channel_count // head_count
    group_count = min(head_count, devices)
    part_count = devices // group_count
    group_heads = head_count // group_count
    part_rows = token_count // part_count
    width = group_heads * head_dim
    selector = step_index[0] % 2
    blend = blend_of(step_index[0])
    limits = block_limits(block_exponents)[..., None]
    residual = (current_pairs.astype(jnp.float32) - earlier_pairs.astype(jnp.float32)).reshape(
        layer_count, 2, token_count, head_count, head_dim
    )
    update = jnp.clip(residual, -limits, limits).astype(jnp.bfloat16)
    pieces = update.reshape(layer_count, 2, part_count, part_rows, group_count, width)
    pieces = pieces.transpose(0, 4, 2, 1, 3, 5).reshape(
        layer_count, devices, 2 * part_rows, width
    )
    asked = queries.reshape(layer_count, token_count, group_count, 1, width)
    asked = jnp.broadcast_to(
        asked.transpose(0, 2, 3, 1, 4),
        (layer_count, group_count, part_count, token_count, width),
    ).reshape(layer_count, devices, token_count, width)
    attended_list = []
    renewed_list = []
    for layer in range(layer_count):
        refresh = selector != layer % 2
        outgoing = jnp.where(refresh, pieces[layer], jnp.zeros_like(pieces[layer]))
        arrived = exchange(jnp.concatenate([outgoing, asked[layer]], 1))
        arrived_update = arrived[:, : 2 * part_rows].reshape(devices, 2, part_rows, width)
        renewed = (
            stale_cache[layer, :, 0].astype(jnp.float32)
            + blend * arrived_update.transpose(1, 0, 2, 3).astype(jnp.float32)
        ).astype(jnp.bfloat16)
        key_rows = renewed[0].reshape(devices * part_rows, group_heads, head_dim)
        value_rows = renewed[1].reshape(devices * part_rows, group_heads, head_dim)
        block_span = 1
        while (
            block_span * token_count < 512 and devices % (2 * block_span) == 0
        ):
            block_span = block_span * 2
        blocks = arrived[:, 2 * part_rows :].reshape(
            devices // block_span, block_span * token_count, group_heads, head_dim
        )
        partial_out, log_total = answer_part(blocks, key_rows, value_rows)
        back_out = exchange(
            partial_out.astype(jnp.bfloat16).reshape(devices, token_count, width)
        ).astype(jnp.float32)
        back_log = exchange(
            log_total.astype(jnp.bfloat16).reshape(devices, token_count, group_heads)
        ).astype(jnp.float32)
        back_out = back_out.reshape(group_count, part_count, token_count, group_heads, head_dim)
        back_log = back_log.reshape(group_count, part_count, token_count, group_heads)
        factor = jnp.exp(back_log - jnp.max(back_log, 1, keepdims=True))
        merged = jnp.sum(factor[..., None] * back_out, 1) / jnp.sum(factor, 1)[..., None]
        attended_list.append(
            merged.transpose(1, 0, 2, 3)
            .reshape(token_count, channel_count)
            .astype(jnp.bfloat16)
        )
        renewed_list.append(renewed)
    return jnp.stack(attended_list), jnp.stack(renewed_list)[:, :, None]


def body(queries, current_pairs, earlier_pairs, stale_cache, block_exponents, step_index):
    layer_count = queries.shape[0]
    head_count = block_exponents.shape[-1]
    devices = lax.axis_size("patch")
    one_part = 1 < devices <= head_count and devices & (devices - 1) == 0 and layer_count == 2
    chosen = whole_key_body if one_part else split_key_body
    return chosen(
        queries, current_pairs, earlier_pairs, stale_cache, block_exponents, step_index
    )


def solution(mesh):
    in_specs = (
        P(None, ("groups", "patch"), None),
        P(None, None, ("groups", "patch"), None),
        P(None, None, ("groups", "patch"), None),
        P(None, None, ("groups", "patch"), None, None, None),
        P(None, None, ("groups", "patch"), None),
        P("groups"),
    )
    out_specs = (
        P(None, ("groups", "patch"), None),
        P(None, None, ("groups", "patch"), None, None, None),
    )
    return jax.shard_map(body, mesh=mesh, in_specs=in_specs, out_specs=out_specs, check_vma=False)
```

```python
from functools import partial

import jax
import jax.numpy as jnp
from jax import lax
from jax.experimental import pallas as pl
from jax.experimental.pallas import tpu as pltpu
from jax.sharding import PartitionSpec as P

STEPS = 50
SATURATION = 448
TOP_LEVEL = 8
VMEM_BYTES = 40 * 1024 * 1024
PACK_BYTES = 60 * 1024 * 1024


def block_limits(exponents):
    return ((SATURATION << TOP_LEVEL) >> exponents).astype(jnp.float32) * (2.0**-TOP_LEVEL)


def blend_of(step):
    return 1.0 - step.astype(jnp.float32) / (2.0 * STEPS)


def layers_of(step):
    kept = lax.rem(step, 2)
    return kept, 1 - kept


def pairwise(array, distance, devices):
    pairs = [(device, device ^ distance) for device in range(devices)]
    return lax.ppermute(array, "patch", pairs)


def start_all(copies):
    for copy in copies:
        copy.start()
    return copies


def wait_all(copies):
    for copy in copies:
        copy.wait()


def pack_kernel(order, step_ref, query_ref, current_ref, earlier_ref, exponent_ref, *refs):
    chips = len(order)
    messages = refs[:chips]
    queries, current, earlier, exponents, limits, sems, side_sems = refs[chips:]
    _, _, channel_count = query_ref.shape
    head_count = exponent_ref.shape[-1]
    head_dim = channel_count // head_count
    width = channel_count // chips
    kept, refreshed = layers_of(step_ref[0])
    here = lax.div(lax.axis_index("patch"), 2)
    copies = start_all(
        [
            pltpu.make_async_copy(exponent_ref.at[refreshed], exponents, sems.at[0]),
            pltpu.make_async_copy(query_ref, queries, sems.at[1]),
        ]
    )
    pair_copies = start_all(
        [
            pltpu.make_async_copy(source.at[refreshed], target, side_sems.at[index])
            for index, (source, target) in enumerate(
                ((current_ref, current), (earlier_ref, earlier))
            )
        ]
    )
    copies[0].wait()
    for side in range(2):
        values = block_limits(exponents[side])
        for head in range(head_count):
            limits[side, :, head * head_dim : (head + 1) * head_dim] = jnp.broadcast_to(
                values[:, head : head + 1], (values.shape[0], head_dim)
            )
    copies[1].wait()
    spans = [
        pl.ds(pl.multiple_of(lax.bitwise_xor(here, chip) * width, width), width)
        for chip in order
    ]
    for chip, span in zip(order, spans):
        for slot, layer in enumerate((kept, refreshed)):
            messages[chip][:, slot * width : (slot + 1) * width] = queries[layer, :, span]
    for side in range(2):
        if side == 0:
            wait_all(pair_copies)
        for chip, span in zip(order, spans):
            residual = current[side, :, span].astype(jnp.float32) - earlier[
                side, :, span
            ].astype(jnp.float32)
            limit = limits[side, :, span]
            update = jnp.minimum(jnp.maximum(residual, -limit), limit).astype(jnp.bfloat16)
            messages[chip][:, (2 + side) * width : (3 + side) * width] = update


def pack(step_index, queries, current_pairs, earlier_pairs, block_exponents, order):
    _, token_count, channel_count = queries.shape
    chips = len(order)
    columns = 4 * (channel_count // chips)
    far = pl.BlockSpec(memory_space=pl.ANY)
    layers = [current_pairs, earlier_pairs, block_exponents]
    return pl.pallas_call(
        partial(pack_kernel, order),
        in_specs=[pl.BlockSpec(memory_space=pltpu.SMEM)] + [far] * 4,
        out_specs=[pl.BlockSpec(memory_space=pltpu.VMEM)] * chips,
        out_shape=[jax.ShapeDtypeStruct((token_count, columns), jnp.bfloat16)] * chips,
        scratch_shapes=[pltpu.VMEM(queries.shape, queries.dtype)]
        + [pltpu.VMEM(array.shape[1:], array.dtype) for array in layers]
        + [
            pltpu.VMEM(current_pairs.shape[1:], jnp.float32),
            pltpu.SemaphoreType.DMA((2,)),
            pltpu.SemaphoreType.DMA((2,)),
        ],
        compiler_params=pltpu.CompilerParams(vmem_limit_bytes=PACK_BYTES),
    )(step_index, queries, current_pairs, earlier_pairs, block_exponents)


def stacked(blocks):
    return jnp.concatenate([block.astype(jnp.float32) for block in blocks], 0).astype(
        jnp.bfloat16
    )


def answer(queries, keys, values, head_dim):
    spans = [
        slice(first, first + head_dim) for first in range(0, queries.shape[-1], head_dim)
    ]
    scores = [
        lax.dot_general(
            queries[:, span],
            keys[:, span],
            (((1,), (1,)), ((), ())),
            preferred_element_type=jnp.float32,
        )
        for span in spans
    ]
    weights = [
        jnp.exp((score - jnp.max(score, -1, keepdims=True)) * head_dim ** (-0.5))
        for score in scores
    ]
    return [
        jnp.dot(weight.astype(jnp.bfloat16), values[:, span], preferred_element_type=jnp.float32)
        / jnp.sum(weight, -1, keepdims=True)
        for weight, span in zip(weights, spans)
    ]


def kept_kernel(order, head_dim, step_ref, query_ref, *refs):
    messages = dict(zip([chip for chip in order if chip], refs))
    own_ref, other_ref, out_ref = refs[len(messages) :]
    token_count = query_ref.shape[1]
    width = own_ref.shape[-1]
    kept, _ = layers_of(step_ref[0])
    here, core = lax.div(lax.axis_index("patch"), 2), lax.rem(lax.axis_index("patch"), 2)
    for group, cache_ref in ((core, own_ref), (1 - core, other_ref)):
        first = pl.multiple_of(group * width, width)
        blocks = []
        for chip in order:
            if chip:
                blocks.append(messages[chip][:, pl.ds(first, width)])
            else:
                place = pl.multiple_of((2 * here + group) * width, width)
                blocks.append(query_ref[kept, :, pl.ds(place, width)])
        queries = stacked(blocks)
        keys, values = cache_ref[kept, 0], cache_ref[kept, 1]
        for head, result in enumerate(answer(queries, keys, values, head_dim)):
            place = pl.ds(pl.multiple_of(first + head * head_dim, head_dim), head_dim)
            for slot in range(len(order)):
                out_ref[slot, :, place] = result[
                    slot * token_count : (slot + 1) * token_count
                ].astype(jnp.bfloat16)


def attend_kept(step_index, queries, arrived, order, stale, other_stale, head_dim):
    chips = len(order)
    messages = [arrived[chip] for chip in order if chip]
    _, token_count, channel_count = queries.shape
    whole = pl.BlockSpec(memory_space=pltpu.VMEM)
    return pl.pallas_call(
        partial(kept_kernel, order, head_dim),
        in_specs=[pl.BlockSpec(memory_space=pltpu.SMEM)] + [whole] * (chips + 2),
        out_specs=whole,
        out_shape=jax.ShapeDtypeStruct(
            (chips, token_count, channel_count // chips), jnp.bfloat16
        ),
        compiler_params=pltpu.CompilerParams(vmem_limit_bytes=VMEM_BYTES),
    )(step_index, queries, *messages, stale, other_stale)


def refreshed_kernel(order, head_dim, step_ref, *refs):
    chips = len(order)
    messages, relayed = refs[:chips], refs[chips : 2 * chips]
    kept_out, own_ref, other_ref = refs[2 * chips : 2 * chips + 3]
    answers = refs[2 * chips + 3 : 3 * chips + 3]
    renewed, updates = refs[3 * chips + 3 :]
    width = own_ref.shape[-1]
    token_count = messages[0].shape[0]
    step = step_ref[0]
    _, refreshed = layers_of(step)
    blend = blend_of(step)
    me = lax.axis_index("patch")
    core = lax.rem(me, 2)
    for slot, chip in enumerate(order):
        for source, message in ((2 * chip, messages[slot]), (2 * chip + 1, relayed[slot])):
            row = pl.multiple_of(lax.bitwise_xor(me, source) * token_count, 8)
            updates[pl.ds(row, token_count), :] = message[:, 4 * width :].astype(jnp.float32)
    results = []
    for turn, (group, cache_ref) in enumerate(((core, own_ref), (1 - core, other_ref))):
        pair = []
        for side in range(2):
            place = pl.ds(pl.multiple_of((2 * side + group) * width, width), width)
            rows = (
                cache_ref[refreshed, side].astype(jnp.float32)
                + blend * updates[:, place]
            ).astype(jnp.bfloat16)
            if turn == 0:
                renewed[side] = rows
            pair.append(rows)
        keys, values = pair
        first = pl.multiple_of(group * width, width)
        queries = stacked(
            [message[:, pl.ds(pl.multiple_of(2 * width + first, width), width)] for message in messages]
        )
        for head, result in enumerate(answer(queries, keys, values, head_dim)):
            place = pl.ds(
                pl.multiple_of(2 * width + first + head * head_dim, head_dim), head_dim
            )
            for slot in range(chips):
                answers[slot][:, place] = result[
                    slot * token_count : (slot + 1) * token_count
                ].astype(jnp.bfloat16)
    for slot in range(chips):
        answers[slot][:, : 2 * width] = kept_out[slot]


def attend_refreshed(
    step_index, messages, relayed, order, kept_out, stale, other_stale, head_dim
):
    chips = len(messages)
    token_count, columns = messages[0].shape
    whole = pl.BlockSpec(memory_space=pltpu.VMEM)
    *answers, renewed = pl.pallas_call(
        partial(refreshed_kernel, order, head_dim),
        in_specs=[pl.BlockSpec(memory_space=pltpu.SMEM)] + [whole] * (2 * chips + 3),
        out_specs=[whole] * (chips + 1),
        out_shape=[jax.ShapeDtypeStruct((token_count, columns // 2), jnp.bfloat16)] * chips
        + [jax.ShapeDtypeStruct(stale.shape[1:], jnp.bfloat16)],
        scratch_shapes=[pltpu.VMEM((stale.shape[2], columns // 2), jnp.float32)],
        compiler_params=pltpu.CompilerParams(vmem_limit_bytes=VMEM_BYTES),
    )(step_index, *messages, *relayed, kept_out, stale, other_stale)
    return answers, renewed


def store_kernel(step_ref, stale_ref, renewed_ref, out_ref, sems):
    kept, refreshed = layers_of(step_ref[0])
    wait_all(
        start_all(
            [
                pltpu.make_async_copy(stale_ref.at[kept], out_ref.at[kept], sems.at[0]),
                pltpu.make_async_copy(renewed_ref, out_ref.at[refreshed], sems.at[1]),
            ]
        )
    )


def store(step_index, stale, renewed):
    far = pl.BlockSpec(memory_space=pl.ANY)
    return pl.pallas_call(
        store_kernel,
        in_specs=[pl.BlockSpec(memory_space=pltpu.SMEM)]
        + [pl.BlockSpec(memory_space=pltpu.VMEM)] * 2,
        out_specs=far,
        out_shape=jax.ShapeDtypeStruct(stale.shape, stale.dtype),
        scratch_shapes=[pltpu.SemaphoreType.DMA((2,))],
        compiler_params=pltpu.CompilerParams(vmem_limit_bytes=VMEM_BYTES),
    )(step_index, stale, renewed)


def after(array, *others):
    return lax.optimization_barrier((array, *others))[0]


def place_kernel(order, step_ref, *refs):
    *answers, out_ref = refs
    width = answers[0].shape[-1] // 2
    here = lax.div(lax.axis_index("patch"), 2)
    for half, layer in enumerate(layers_of(step_ref[0])):
        for slot, chip in enumerate(order):
            first = pl.multiple_of(lax.bitwise_xor(here, chip) * width, width)
            out_ref[layer, :, pl.ds(first, width)] = answers[slot][
                :, half * width : (half + 1) * width
            ]


def place(step_index, answers, order):
    token_count, columns = answers[0].shape
    attended = jax.ShapeDtypeStruct((2, token_count, len(order) * columns // 2), jnp.bfloat16)
    return pl.pallas_call(
        partial(place_kernel, order),
        in_specs=[pl.BlockSpec(memory_space=pltpu.SMEM)]
        + [pl.BlockSpec(memory_space=pltpu.VMEM)] * len(order),
        out_specs=pl.BlockSpec(memory_space=pltpu.VMEM),
        out_shape=attended,
        compiler_params=pltpu.CompilerParams(vmem_limit_bytes=VMEM_BYTES),
    )(step_index, *answers)


def distances(chips):
    if chips == 8:
        return [5, 3, 4, 6, 2, 1, 7, 0], [7, 6, 4, 5, 3, 2, 1, 0]
    order = list(range(chips - 1, -1, -1))
    return order, order


def whole_key_body(
    queries, current_pairs, earlier_pairs, stale_cache, block_exponents, step_index
):
    devices = lax.axis_size("patch")
    chips = devices // 2
    layer_count, token_count, channel_count = queries.shape
    head_dim = channel_count // block_exponents.shape[-1]
    stale = stale_cache.reshape(layer_count, 2, devices * token_count, -1)
    order, back_order = distances(chips)
    other_stale = pairwise(stale, 1, devices)
    messages = pack(
        step_index, queries, current_pairs, earlier_pairs, block_exponents, order
    )
    *messages, other_stale = lax.optimization_barrier((*messages, other_stale))
    arrived = {
        chip: pairwise(messages[chip], 2 * chip, devices) for chip in order if chip
    }
    arrived[0] = messages[0]
    kept_out = attend_kept(
        step_index, queries, arrived, order, stale, other_stale, head_dim
    )
    arrived = [arrived[chip] for chip in order]
    relayed = [pairwise(message, 1, devices) for message in arrived]
    answers, renewed = attend_refreshed(
        step_index, arrived, relayed, order, kept_out, stale, other_stale, head_dim
    )
    by_chip = [answers[order.index(chip)] for chip in range(chips)]
    returned = [
        pairwise(by_chip[chip], 2 * chip, devices) if chip else by_chip[0] for chip in back_order
    ]
    renewed = store(step_index, stale, after(renewed, returned[0]))
    attended = place(step_index, returned, back_order)
    return attended, renewed.reshape(stale_cache.shape)


def exchange(rows):
    return lax.all_to_all(rows, "patch", split_axis=0, concat_axis=0, tiled=True)


def answer_part(blocks, key_rows, value_rows):
    score_scale = key_rows.shape[-1] ** (-0.5)

    def one_block(query_block):
        scores = (
            jnp.einsum("qhd,khd->hqk", query_block, key_rows, preferred_element_type=jnp.float32)
            * score_scale
        )
        peak = jnp.max(scores, -1, keepdims=True)
        weights = jnp.exp(scores - peak)
        total = jnp.sum(weights, -1)
        mixed = jnp.einsum(
            "hqk,khd->qhd",
            weights.astype(jnp.bfloat16),
            value_rows,
            preferred_element_type=jnp.float32,
        )
        return mixed / total.T[..., None], (peak[..., 0] + jnp.log(total)).T

    return lax.map(one_block, blocks)


def split_key_body(
    queries, current_pairs, earlier_pairs, stale_cache, block_exponents, step_index
):
    devices = lax.axis_size("patch")
    layer_count, token_count, channel_count = queries.shape
    head_count = block_exponents.shape[-1]
    head_dim = channel_count // head_count
    group_count = min(head_count, devices)
    part_count = devices // group_count
    group_heads = head_count // group_count
    part_rows = token_count // part_count
    width = group_heads * head_dim
    selector = step_index[0] % 2
    blend = blend_of(step_index[0])
    limits = block_limits(block_exponents)[..., None]
    residual = (current_pairs.astype(jnp.float32) - earlier_pairs.astype(jnp.float32)).reshape(
        layer_count, 2, token_count, head_count, head_dim
    )
    update = jnp.clip(residual, -limits, limits).astype(jnp.bfloat16)
    pieces = update.reshape(layer_count, 2, part_count, part_rows, group_count, width)
    pieces = pieces.transpose(0, 4, 2, 1, 3, 5).reshape(
        layer_count, devices, 2 * part_rows, width
    )
    asked = queries.reshape(layer_count, token_count, group_count, 1, width)
    asked = jnp.broadcast_to(
        asked.transpose(0, 2, 3, 1, 4),
        (layer_count, group_count, part_count, token_count, width),
    ).reshape(layer_count, devices, token_count, width)
    attended_list = []
    renewed_list = []
    for layer in range(layer_count):
        refresh = selector != layer % 2
        outgoing = jnp.where(refresh, pieces[layer], jnp.zeros_like(pieces[layer]))
        arrived = exchange(jnp.concatenate([outgoing, asked[layer]], 1))
        arrived_update = arrived[:, : 2 * part_rows].reshape(devices, 2, part_rows, width)
        renewed = (
            stale_cache[layer, :, 0].astype(jnp.float32)
            + blend * arrived_update.transpose(1, 0, 2, 3).astype(jnp.float32)
        ).astype(jnp.bfloat16)
        key_rows = renewed[0].reshape(devices * part_rows, group_heads, head_dim)
        value_rows = renewed[1].reshape(devices * part_rows, group_heads, head_dim)
        block_span = 1
        while (
            block_span * token_count < 512 and devices % (2 * block_span) == 0
        ):
            block_span = block_span * 2
        blocks = arrived[:, 2 * part_rows :].reshape(
            devices // block_span, block_span * token_count, group_heads, head_dim
        )
        partial_out, log_total = answer_part(blocks, key_rows, value_rows)
        back_out = exchange(
            partial_out.astype(jnp.bfloat16).reshape(devices, token_count, width)
        ).astype(jnp.float32)
        back_log = exchange(
            log_total.astype(jnp.bfloat16).reshape(devices, token_count, group_heads)
        ).astype(jnp.float32)
        back_out = back_out.reshape(group_count, part_count, token_count, group_heads, head_dim)
        back_log = back_log.reshape(group_count, part_count, token_count, group_heads)
        factor = jnp.exp(back_log - jnp.max(back_log, 1, keepdims=True))
        merged = jnp.sum(factor[..., None] * back_out, 1) / jnp.sum(factor, 1)[..., None]
        attended_list.append(
            merged.transpose(1, 0, 2, 3)
            .reshape(token_count, channel_count)
            .astype(jnp.bfloat16)
        )
        renewed_list.append(renewed)
    return jnp.stack(attended_list), jnp.stack(renewed_list)[:, :, None]


def body(queries, current_pairs, earlier_pairs, stale_cache, block_exponents, step_index):
    layer_count = queries.shape[0]
    head_count = block_exponents.shape[-1]
    devices = lax.axis_size("patch")
    one_part = 1 < devices <= head_count and devices & (devices - 1) == 0 and layer_count == 2
    chosen = whole_key_body if one_part else split_key_body
    return chosen(
        queries, current_pairs, earlier_pairs, stale_cache, block_exponents, step_index
    )


def solution(mesh):
    in_specs = (
        P(None, ("groups", "patch"), None),
        P(None, None, ("groups", "patch"), None),
        P(None, None, ("groups", "patch"), None),
        P(None, None, ("groups", "patch"), None, None, None),
        P(None, None, ("groups", "patch"), None),
        P("groups"),
    )
    out_specs = (
        P(None, ("groups", "patch"), None),
        P(None, None, ("groups", "patch"), None, None, None),
    )
    return jax.shard_map(body, mesh=mesh, in_specs=in_specs, out_specs=out_specs, check_vma=False)
```
